128 devices in a mesh: member: 8 (over y_lo, z), region: 16 (over x, y_hi, core).
Axes of the slice: x: 4, y: 4 (y_hi: 2, y_lo: 2; y = y_hi * 2 + y_lo), z: 4, core: 2. Of those that a mesh axis runs over, the one named last changes fastest.
Arguments:
- latent_vertex_values: bfloat16 [64, 8192, 512], P('member', 'region'), may hold values from -6 to 6
- background_field: bfloat16 [64, 16384, 128], P('member', 'region'), may hold values from -6 to 6
- edge_senders: int32 [8192, 6], P('region'), may hold values from 448 to 1087, as said below
- grid_parent: int32 [16384], P('region'), may hold values from 0 to 511
- w_send: bfloat16 [512, 512], replicated, may hold values from -0.25 to 0.25
- w_recv: bfloat16 [512, 512], replicated, may hold values from -0.25 to 0.25
- w_node: bfloat16 [512, 512], replicated, may hold values from -0.25 to 0.25
- w_agg: bfloat16 [512, 512], replicated, may hold values from -0.109375 to 0.109375
- w_out: bfloat16 [512, 512], replicated, may hold values from -0.25 to 0.25
- norm_gain: float32 [512], replicated, may hold values from 0.25 to 1.75
- w_dec: bfloat16 [512, 128], replicated, may hold values from -0.25 to 0.25
- obs_loc: int32 [32768], P(('member', 'region')), may hold values from 0 to 16383
- obs_count: int32 [128], P(('member', 'region')), may hold values from 1 to 256, 16384 in all
- obs_value: float32 [32768], P(('member', 'region')), may hold values from -6 to 6
- obs_var: float32 [32768], P(('member', 'region')), may hold values from 0.25 to 4
- obs_nbr: int32 [32, 16384], P(None, ('member', 'region')), may hold values from 0 to 767
- loc_weight: float32 [32, 16384], P(None, ('member', 'region')), may hold values from 0.1 to 1
Outputs:
- processed_vertex_values: bfloat16 [64, 8192, 512], P('member', 'region')
- assimilated_field: bfloat16 [64, 16384, 128], P('member', 'region')
The draws below stay inside these ranges and needn't reach their ends.
Inputs may be any that keep to these rules, and one draw needn't show every extreme that they name: edge_senders[n, e] indexes the extended rows of n's region (the 512 nodes of the previous region, its own, then those of the next region, regions in a cycle); an entry outside the own region lies in the last 64 nodes of the previous region or the first 64 nodes of the next. `grid_parent`: a node of the grid point's own region. `obs_loc`: c * 128 + p: channel c at point p of the slot's tile. A tile's live observations are its first obs_count slots. `obs_nbr`: indexes the extended slots of the point's tile: the previous tile's, its own, then the next tile's.
All inputs are finite; a program needn't handle non-finite values. No bound on the sum of `obs_count` on one device may be relied on, other than what follows from the above.
Results may differ from the reference program's by a relative error of at most 0.008.
Values may be sent and summed in bfloat16 or wider, within the bound.
No kernel may reach another device: no remote copies, remote signals or barrier semaphores. Data moves between devices by JAX's collectives and lax.ppermute only.
A program may use at most 128 MiB of HBM per device.

```python
import math
import jax
import jax.numpy as jnp
import numpy as np
from jax import lax

WIDTH = 512
FIELD_VARIABLES = 128
ENSEMBLE_SIZE = 64
DEGREE = 6
RIM = 64
LOCAL_OBS = 32
NS_ITERS = 6
NODE_DEV = 512
PATCH_LOCATIONS = 128
OBS_MAX = 256
NODES = 8192
GRID_R = 1024
GRID = 16384
PATCH_SHARE = 8
N_REGION = 16
DEVICES = 128


def draw_edge_senders(key, part):
    key = jax.random.fold_in(key, 11)
    key_kind, key_own, key_prev, key_next = jax.random.split(key, 4)
    shape = (NODES, DEGREE)
    kind = jax.random.randint(key_kind, shape, 0, 8)
    own = jax.random.randint(key_own, shape, NODE_DEV, 2 * NODE_DEV)
    before = jax.random.randint(key_prev, shape, NODE_DEV - RIM, NODE_DEV)
    after = jax.random.randint(key_next, shape, 2 * NODE_DEV, 2 * NODE_DEV + RIM)
    result = jnp.where(kind == 0, before, jnp.where(kind == 1, after, own))
    result = result.at[0, 0].set(NODE_DEV - RIM)
    result = result.at[NODES - 1, DEGREE - 1].set(2 * NODE_DEV + RIM - 1)
    return result.astype(jnp.int32)


def set_ends(values, key, low, high):
    longest = values.shape.index(max(values.shape))
    spots = []
    for shift in (0, 1):
        where = [jax.random.randint(jax.random.fold_in(key, axis), (), 0, length) for axis, length in enumerate(values.shape)]
        where[longest] = (where[longest] + shift) % values.shape[longest]
        spots.append(tuple(where))
    return values.at[spots[0]].set(low).at[spots[1]].set(high)


def level_of(key, shape, pieces, low, top_value):
    loudness, own = 1.0, jax.random.fold_in(key, 6)
    for dim, shards_of in pieces:
        heights = jnp.exp(jax.random.uniform(jax.random.fold_in(own, dim), (shards_of,), jnp.float32, low / len(pieces), top_value / len(pieces)))
        loudness = loudness * jnp.repeat(heights, shape[dim] // shards_of).reshape([-1 if axis == dim else 1 for axis in range(len(shape))])
    return loudness


def split_up(amount, total, limit, slope):
    loads = [(1 << 20) // math.isqrt(rank ** slope) + 1 for rank in range(2, amount + 1)]
    surplus, counts = total - limit - (amount - 1), [1] * (amount - 1)
    while surplus > 0:
        candidates = [i for i in range(amount - 1) if counts[i] < limit]
        pool, left = sum([loads[i] for i in candidates]), surplus
        for i in candidates:
            addition = min(limit - counts[i], max(1, left * loads[i] // pool), surplus)
            counts[i] = counts[i] + addition
            surplus = surplus - addition
    return np.array([limit] + counts)


def ragged_sizes(key, number_of, total, most, lean):
    if number_of == 2:
        one = jax.random.randint(key, (), max(1, total - most), min(most, total - 1) + 1)
        return jnp.stack([one, total - one])
    tallies = jnp.asarray(split_up(number_of, total, most, lean), jnp.int32)
    pairs = (number_of - 1) // 2
    giver, sink = tallies[1:1 + 2 * pairs:2], tallies[2:2 + 2 * pairs:2]
    slack = jnp.minimum(giver - 1, most - sink)
    passed = jax.random.randint(jax.random.fold_in(key, 1), (pairs,), 0, 1 << 20) % (slack + 1)
    tallies = tallies.at[1:1 + 2 * pairs:2].set(giver - passed).at[2:2 + 2 * pairs:2].set(sink + passed)
    return tallies[jax.random.permutation(jax.random.fold_in(key, 2), number_of)]


def noise(key, shape, spread, limit, pieces=(), kind=jnp.bfloat16):
    loudness = level_of(key, shape, pieces, -0.22, 0.18) if pieces else 1.0
    drawn = jax.random.normal(key, shape, jnp.float32) * spread * loudness
    return jnp.minimum(jnp.maximum(drawn, -limit), limit).astype(kind)


def setup_inputs(seed: int = 0) -> dict:
    seeds = jax.random.split(jax.random.key(seed), 18)
    return {
        "latent_vertex_values": noise(seeds[0], (ENSEMBLE_SIZE, NODES, WIDTH), 1.0, 6.0, ((0, 8), (1, 16))),
        "background_field": noise(seeds[1], (ENSEMBLE_SIZE, GRID, FIELD_VARIABLES), 1.0, 6.0, ((0, 8), (1, 16))),
        "edge_senders": draw_edge_senders(jax.random.fold_in(seeds[17], 71), 0),
        "grid_parent": set_ends(jax.random.randint(seeds[3], (GRID,), 0, NODE_DEV), jax.random.fold_in(seeds[3], 1), 0, NODE_DEV - 1).astype(jnp.int32),
        "w_send": noise(seeds[4], (WIDTH, WIDTH), WIDTH ** -0.5, 0.25),
        "w_recv": noise(seeds[5], (WIDTH, WIDTH), WIDTH ** -0.5, 0.25),
        "w_node": noise(seeds[6], (WIDTH, WIDTH), WIDTH ** -0.5, 0.25),
        "w_agg": noise(seeds[7], (WIDTH, WIDTH), (WIDTH * DEGREE) ** -0.5, 0.109375),
        "w_out": noise(seeds[8], (WIDTH, WIDTH), WIDTH ** -0.5, 0.25),
        "norm_gain": jnp.clip(1.0 + 0.15 * jax.random.normal(seeds[9], (WIDTH,), jnp.float32), 0.25, 1.75),
        "w_dec": noise(seeds[10], (WIDTH, FIELD_VARIABLES), WIDTH ** -0.5, 0.25),
        "obs_loc": set_ends(jax.random.randint(seeds[11], (DEVICES * OBS_MAX,), 0, FIELD_VARIABLES * PATCH_LOCATIONS), jax.random.fold_in(seeds[11], 1), 0, (FIELD_VARIABLES * PATCH_LOCATIONS) - 1).astype(jnp.int32),
        "obs_count": ragged_sizes(seeds[12], DEVICES, DEVICES * OBS_MAX // 2, OBS_MAX, 2).astype(jnp.int32),
        "obs_value": noise(seeds[13], (DEVICES * OBS_MAX,), 1.0, 6.0, ((0, 128),), jnp.float32),
        "obs_var": jnp.clip(jnp.exp(math.log(4.0) - 2.7725887 * jax.random.uniform(seeds[14], (DEVICES * OBS_MAX,), jnp.float32) ** level_of(seeds[14], (DEVICES * OBS_MAX,), ((0, 128),), -0.2, 0.2)), 0.25, 4.0),
        "obs_nbr": set_ends(jax.random.randint(seeds[15], (LOCAL_OBS, DEVICES * PATCH_LOCATIONS), 0, 3 * OBS_MAX), jax.random.fold_in(seeds[15], 1), 0, (3 * OBS_MAX) - 1).astype(jnp.int32),
        "loc_weight": jnp.clip(0.1 + 0.9 * jax.random.uniform(seeds[16], (LOCAL_OBS, DEVICES * PATCH_LOCATIONS), jnp.float32) ** level_of(seeds[16], (LOCAL_OBS, DEVICES * PATCH_LOCATIONS), ((1, 128),), -0.2, 0.2), 0.1, 1.0),
    }


def layer_norm(values, gain):
    mean = lax.optimization_barrier(jnp.mean(values, axis=-1, keepdims=True))
    centred = values - mean
    var = lax.optimization_barrier(jnp.mean(centred * centred, axis=-1, keepdims=True))
    return centred / jnp.sqrt(var + 1e-05) * gain

def transform(ens, payload, nbr, loc):
    members = ens.shape[0]
    hp = lax.Precision.HIGHEST
    ypert = payload[:members]
    rinv = payload[members]
    dres = payload[members + 1]
    xval = ens.astype(jnp.float32)
    xpert = xval - lax.optimization_barrier(jnp.mean(xval, axis=0, keepdims=True))
    ylocal = ypert[:, nbr]
    wlocal = loc * rinv[nbr]
    dlocal = loc * dres[nbr]
    eye = jnp.eye(members, dtype=jnp.float32)[:, :, None]
    amat = jnp.einsum('ilp,jlp->ijp', ylocal * wlocal[None], ylocal, precision=hp) + (members - 1.0) * eye
    scale = jnp.sqrt(lax.optimization_barrier(jnp.sum(amat * amat, axis=(0, 1))))
    ymat = amat / scale
    zmat = jnp.broadcast_to(eye, amat.shape)
    for step in range(NS_ITERS):
        tmat = 1.5 * eye - 0.5 * jnp.einsum('ijp,jkp->ikp', zmat, ymat, precision=hp)
        ymat = jnp.einsum('ijp,jkp->ikp', ymat, tmat, precision=hp)
        zmat = jnp.einsum('ijp,jkp->ikp', tmat, zmat, precision=hp)
    smat = zmat / jnp.sqrt(scale)
    vec = jnp.einsum('ilp,lp->ip', ylocal, dlocal, precision=hp)
    wbar = jnp.einsum('ijp,jp->ip', smat, jnp.einsum('ijp,jp->ip', smat, vec, precision=hp), precision=hp)
    wmat = wbar[:, None, :] + jnp.sqrt(members - 1.0) * smat
    increment = jnp.einsum('jpc,jkp->kpc', xpert, wmat, precision=hp) - xpert
    return increment.astype(jnp.bfloat16)

def reference(latent_vertex_values, background_field, edge_senders, grid_parent, w_send, w_recv, w_node, w_agg, w_out, norm_gain, w_dec, obs_loc, obs_count, obs_value, obs_var, obs_nbr, loc_weight):
    senders = edge_senders.reshape(N_REGION, NODE_DEV, DEGREE)
    owner = jnp.arange(GRID, dtype=jnp.int32) // GRID_R * NODE_DEV + grid_parent

    def propagate_dynamics(pair):
        state, background_values = pair
        sent = jnp.dot(state, w_send, preferred_element_type=jnp.float32).astype(jnp.bfloat16)
        blocks = sent.reshape(N_REGION, NODE_DEV, WIDTH)
        extended = jnp.concatenate([jnp.roll(blocks, 1, 0), blocks, jnp.roll(blocks, -1, 0)], axis=1)
        gathered = jax.vmap(lambda rows, index: rows[index])(extended, senders).reshape(NODES, DEGREE, WIDTH)
        recv = jnp.dot(state, w_recv, preferred_element_type=jnp.float32)
        agg = lax.optimization_barrier(jnp.sum(jax.nn.silu(gathered.astype(jnp.float32) + recv[:, None, :]), axis=1)).astype(jnp.bfloat16)
        pre = jnp.dot(state, w_node, preferred_element_type=jnp.float32) + jnp.dot(agg, w_agg, preferred_element_type=jnp.float32)
        hidden = jax.nn.silu(pre).astype(jnp.bfloat16)
        out = jnp.dot(hidden, w_out, preferred_element_type=jnp.float32)
        decoded_field = (state.astype(jnp.float32) + layer_norm(out, norm_gain)).astype(jnp.bfloat16)
        decoded = jnp.dot(decoded_field, w_dec, preferred_element_type=jnp.float32)
        predicted_field = (background_values.astype(jnp.float32) + decoded[owner]).astype(jnp.bfloat16)
        return (decoded_field, predicted_field)
    processed_vertex_values, predicted_field = lax.map(propagate_dynamics, (latent_vertex_values, background_field))
    assimilated_patches = predicted_field.reshape(ENSEMBLE_SIZE, N_REGION, DEVICES, PATCH_SHARE, FIELD_VARIABLES).transpose(2, 0, 1, 3, 4).reshape(DEVICES, ENSEMBLE_SIZE, PATCH_LOCATIONS, FIELD_VARIABLES)
    locs = obs_loc.reshape(DEVICES, OBS_MAX)
    flat_index = (locs % PATCH_LOCATIONS * FIELD_VARIABLES + locs // PATCH_LOCATIONS).astype(jnp.int32)
    yens = jax.vmap(lambda ens, index: ens.reshape(ENSEMBLE_SIZE, PATCH_LOCATIONS * FIELD_VARIABLES)[:, index])(assimilated_patches, flat_index).astype(jnp.float32)
    ybar = lax.optimization_barrier(jnp.mean(yens, axis=1))
    ypert = yens - ybar[:, None, :]
    valid = (jnp.arange(OBS_MAX, dtype=jnp.int32)[None, :] < obs_count[:, None]).astype(jnp.float32)
    rinv = valid / obs_var.reshape(DEVICES, OBS_MAX)
    dres = (obs_value.reshape(DEVICES, OBS_MAX) - ybar) * rinv
    payload = jnp.concatenate([ypert, rinv[:, None, :], dres[:, None, :]], axis=1)
    padded = jnp.pad(payload, ((1, 1), (0, 0), (0, 0)))
    extended = jnp.concatenate([padded[:-2], padded[1:-1], padded[2:]], axis=2)
    nbr_tiles = obs_nbr.reshape(LOCAL_OBS, DEVICES, PATCH_LOCATIONS).transpose(1, 0, 2)
    loc_tiles = loc_weight.reshape(LOCAL_OBS, DEVICES, PATCH_LOCATIONS).transpose(1, 0, 2)
    increment = lax.map(lambda item: transform(item[0], item[1], item[2], item[3]), (assimilated_patches, extended, nbr_tiles, loc_tiles))
    homebound_portion = increment.reshape(DEVICES, ENSEMBLE_SIZE, N_REGION, PATCH_SHARE, FIELD_VARIABLES).transpose(1, 2, 0, 3, 4).reshape(ENSEMBLE_SIZE, GRID, FIELD_VARIABLES)
    assimilated_field = (predicted_field.astype(jnp.float32) + homebound_portion.astype(jnp.float32)).astype(jnp.bfloat16)
    return (processed_vertex_values, assimilated_field)
```

```python
import jax
import jax.numpy as jnp
from jax import lax
from jax.experimental import pallas as pl
from jax.experimental.pallas import tpu as pltpu
from jax.sharding import PartitionSpec as P

NS_ITERS = 6
LANES = 128
RIM = 64
F32 = jnp.float32
BF16 = jnp.bfloat16
MR = ("member", "region")
VM = pl.BlockSpec(memory_space=pltpu.VMEM)
SM = pl.BlockSpec(memory_space=pltpu.SMEM)


def dot(a, b):
    return jnp.dot(a, b, preferred_element_type=F32)


def forecast_kernel(
    edge_ref,
    parent_ref,
    latent_ref,
    before_ref,
    after_ref,
    back_ref,
    w_send_ref,
    w_recv_ref,
    w_node_ref,
    w_agg_ref,
    w_out_ref,
    gain_ref,
    w_dec_ref,
    proc_ref,
    fore_ref,
    send_s,
    recv_s,
    dec_s,
    back_s,
):
    members, nodes, width = latent_ref.shape
    cols = width // LANES
    step = cols * members
    rim = before_ref.shape[1]
    degree = edge_ref.shape[0] // nodes
    grid_r = back_ref.shape[1]

    def scatter_rows(ref, first, member, values):
        for c in range(cols):
            ref[pl.ds(first * step + c * members + member, values.shape[0], stride=step), :] = (
                values[:, c * LANES : (c + 1) * LANES]
            )

    def project(m, carry):
        state = latent_ref[m]
        own = dot(state, w_send_ref[...]).astype(BF16).astype(F32) * 0.5
        scatter_rows(send_s, rim, m, own)
        edge = dot(before_ref[m], w_send_ref[...]).astype(BF16).astype(F32) * 0.5
        scatter_rows(send_s, 0, m, edge)
        edge = dot(after_ref[m], w_send_ref[...]).astype(BF16).astype(F32) * 0.5
        scatter_rows(send_s, rim + nodes, m, edge)
        scatter_rows(recv_s, 0, m, dot(state, w_recv_ref[...]) * 0.5)
        back_s[pl.ds(m, grid_r, stride=members), :] = back_ref[m].astype(F32)
        return carry

    lax.fori_loop(0, members, project, 0)

    def aggregate(n, carry):
        mine = recv_s[pl.ds(pl.multiple_of(n * step, step), step), :]
        total = jnp.zeros_like(mine)
        for e in range(degree):
            row = pl.multiple_of(edge_ref[n * degree + e], step)
            half = send_s[pl.ds(row, step), :] + mine
            total = total + (half + half * jnp.tanh(half))
        recv_s[pl.ds(pl.multiple_of(n * step, step), step), :] = total
        return carry

    lax.fori_loop(0, nodes, aggregate, 0, unroll=4)

    def update(m, carry):
        state = latent_ref[m]
        agg = jnp.concatenate(
            [recv_s[pl.ds(c * members + m, nodes, stride=step), :] for c in range(cols)], axis=1
        ).astype(BF16)
        pre = (dot(state, w_node_ref[...]) + dot(agg, w_agg_ref[...])) * 0.5
        hidden = (pre + pre * jnp.tanh(pre)).astype(BF16)
        out = dot(hidden, w_out_ref[...])
        mean = jnp.mean(out, axis=-1, keepdims=True)
        centred = out - mean
        var = jnp.mean(centred * centred, axis=-1, keepdims=True)
        norm = centred * lax.rsqrt(var + 1e-05) * gain_ref[...]
        proc = (state.astype(F32) + norm).astype(BF16)
        proc_ref[m] = proc
        dec_s[pl.ds(m, nodes, stride=members), :] = dot(proc, w_dec_ref[...])
        return carry

    lax.fori_loop(0, members, update, 0)

    share = fore_ref.shape[1] // members

    def spread(t, carry):
        rows = [
            dec_s[pl.ds(pl.multiple_of(parent_ref[t * share + q], members), members), :]
            for q in range(share)
        ]
        fore_ref[t] = (jnp.concatenate(rows, axis=0) + back_s[pl.ds(t * share * members, share * members), :]).astype(BF16)
        return carry

    lax.fori_loop(0, fore_ref.shape[0], spread, 0, unroll=2)


def forecast(latent, before, after, back, senders, parent, weights):
    members, nodes, width = latent.shape
    grid_r = back.shape[1]
    rim = before.shape[1]
    step = members * width // LANES
    tiles = lax.axis_size("member") * lax.axis_size("region")
    edge = ((senders - (nodes - rim)) * step).reshape(-1)
    return pl.pallas_call(
        forecast_kernel,
        out_shape=(
            jax.ShapeDtypeStruct(latent.shape, BF16),
            jax.ShapeDtypeStruct((tiles, members * grid_r // tiles, LANES), BF16),
        ),
        in_specs=[SM, SM] + [VM] * 11,
        out_specs=(VM, VM),
        scratch_shapes=[
            pltpu.VMEM(((nodes + 2 * rim) * step, LANES), F32),
            pltpu.VMEM((nodes * step, LANES), F32),
            pltpu.VMEM((nodes * members, LANES), F32),
            pltpu.VMEM((grid_r * members, LANES), F32),
        ],
        compiler_params=pltpu.CompilerParams(vmem_limit_bytes=60 * 2**20),
        name="forecast",
    )(edge, parent * members, latent, before, after, back, *weights)


def observe_kernel(loc_ref, count_ref, ens_ref, value_ref, var_ref, pay_ref):
    groups, regions, rows, _ = ens_ref.shape
    size = 8
    members = groups * size
    slots = loc_ref.shape[0]
    lane = lax.broadcasted_iota(jnp.int32, (members, LANES), 1)
    for part in range(slots // LANES):

        def take(i, acc):
            loc = loc_ref[part * LANES + i]
            point, channel = loc % LANES, loc // LANES
            region, place = point // size, point % size
            start = pl.multiple_of(place // 2 * 2 * size, 2 * size)
            second = place % 2
            pieces = []
            for g in range(groups):
                pair = ens_ref[g, region, pl.ds(start, 2 * size), :].astype(F32)
                pieces.append(jnp.where(second == 1, pair[size:], pair[:size]))
            block = jnp.concatenate(pieces, axis=0)
            turned = pltpu.roll(block, (i - channel + LANES) % LANES, 1)
            return jnp.where(lane == i, turned, acc)

        yens = lax.fori_loop(0, LANES, take, jnp.zeros((members, LANES), F32), unroll=2)
        span = slice(part * LANES, (part + 1) * LANES)
        ybar = jnp.mean(yens, axis=0, keepdims=True)
        slot = lax.broadcasted_iota(jnp.int32, (1, LANES), 1) + part * LANES
        rinv = jnp.where(slot < count_ref[0], 1.0, 0.0) / var_ref[:, span]
        dres = (value_ref[:, span] - ybar) * rinv
        row = lax.broadcasted_iota(jnp.int32, (16, LANES), 0)
        extra = jnp.where(row == 0, rinv, jnp.where(row == 1, dres, 0.0))
        pay_ref[0:members, span] = (yens - ybar).astype(BF16)
        pay_ref[members : members + 16, span] = extra.astype(BF16)


def observe(ens, loc, count, value, var):
    groups, regions, rows, _ = ens.shape
    return pl.pallas_call(
        observe_kernel,
        out_shape=jax.ShapeDtypeStruct((groups * 8 + 16, loc.shape[0]), BF16),
        in_specs=[SM, SM, VM, VM, VM],
        out_specs=VM,
        compiler_params=pltpu.CompilerParams(vmem_limit_bytes=40 * 2**20),
        name="observe",
    )(loc, count, ens, value[None], var[None])


def analyse_kernel(
    before_ref,
    own_ref,
    after_ref,
    nbr_ref,
    loc_ref,
    ens_ref,
    inc_ref,
    pay_s,
    bl_s,
    bk_s,
    g_s,
    m_s,
    r_s,
    q_s,
    t_s,
    c_s,
    v_s,
    w_s,
):
    groups, regions, rows, _ = ens_ref.shape
    size = 8
    members = groups * size
    order = nbr_ref.shape[0]
    nb = order // size
    slots = own_ref.shape[1]
    parts = slots // LANES
    sub = lax.broadcasted_iota(jnp.int32, (size, LANES), 0)

    for i, ref in enumerate((before_ref, own_ref, after_ref)):
        for h in range(parts):
            pay_s[i * parts + h] = ref[0 : members + 16, h * LANES : (h + 1) * LANES].astype(F32)

    def full(row):
        return jnp.broadcast_to(row, (size, LANES))

    def gather(l, vec):
        index = nbr_ref[pl.ds(l, 1), :]
        lane = full(index % LANES)
        panel = full(index // LANES)
        masks = [panel == j for j in range(1, 3 * parts)]

        def pick(first):
            out = None
            for j in range(3 * parts):
                got = jnp.take_along_axis(
                    pay_s[j, pl.ds(first, size), :], lane, axis=1, mode="promise_in_bounds"
                )
                out = got if out is None else jnp.where(masks[j - 1], got, out)
            return out

        extra = pick(members)
        weight = loc_ref[pl.ds(l, 1), :]
        root = jnp.sqrt(weight * extra[0:1])
        dl = weight * extra[1:2]
        new = []
        for g in range(groups):
            yl = pick(g * size)
            new.append(vec[g] + yl * dl)
            b = yl * root
            bl_s[pl.ds(pl.multiple_of(l * members + g * size, size), size), :] = b
            bk_s[pl.ds(g * size * order + l, size, stride=order), :] = b
        return tuple(new)

    zero = jnp.zeros((size, LANES), F32)
    vec = lax.fori_loop(0, order, gather, tuple([zero] * groups))

    def row_of(ref, r):
        return jnp.broadcast_to(ref[pl.ds(r, 1), :], (size, LANES))

    def symmetric(count, left, right, left_step, finish):
        for a in range(nb):
            width = nb - a

            def body(k, acc):
                rhs = [
                    right[pl.ds(pl.multiple_of(k * order + (a + j) * size, size), size), :]
                    for j in range(width)
                ]
                out = []
                for i in range(size):
                    lhs = row_of(left, k * left_step + a * size + i)
                    for j in range(width):
                        out.append(acc[i * width + j] + lhs * rhs[j])
                return tuple(out)

            acc = lax.fori_loop(0, count, body, tuple([zero] * (size * width)), unroll=2)
            for i in range(size):
                for j in range(width):
                    finish(a * size + i, a + j, acc[i * width + j])

    def at(ref, i, jb):
        return ref[pl.ds(i * order + jb * size, size), :]

    def put(ref, i, jb, value):
        ref[pl.ds(i * order + jb * size, size), :] = value
        if jb != i // size:
            ref[pl.ds(jb * size * order + i, size, stride=order), :] = value

    symmetric(members, bk_s, bk_s, order, lambda i, jb, v: put(g_s, i, jb, v))

    square, trace = zero, zero
    for i in range(order):
        for jb in range(nb):
            g = at(g_s, i, jb)
            square = square + g * g
            if jb == i // size:
                trace = trace + jnp.where(sub == i % size, g, 0.0)
    base = members - 1.0
    total = (
        base * base * members
        + 2.0 * base * jnp.sum(trace, axis=0, keepdims=True)
        + jnp.sum(square, axis=0, keepdims=True)
    )
    scale = jnp.sqrt(total)
    inv = 1.0 / scale
    a_coef = full(base * inv)

    z = 1.5 - 0.5 * a_coef
    for i in range(order):
        for jb in range(nb):
            g = at(g_s, i, jb) * inv
            g_s[pl.ds(i * order + jb * size, size), :] = g
            if jb == i // size:
                here = sub == i % size
                m = jnp.where(here, -0.5, 0.0)
                r = jnp.where(here, z, 0.0) - 0.5 * g
            else:
                m = zero
                r = -0.5 * g
            m_s[pl.ds(i * order + jb * size, size), :] = m
            r_s[pl.ds(i * order + jb * size, size), :] = r
            q_s[pl.ds(i * order + jb * size, size), :] = a_coef * m + r

    for it in range(1, NS_ITERS):
        last = it == NS_ITERS - 1
        t = 1.5 - 0.5 * a_coef * z * z

        def tmat(i, jb, v):
            q, r = at(q_s, i, jb), at(r_s, i, jb)
            put(t_s, i, jb, -0.5 * (v + z * (q - r)))

        symmetric(order, q_s, r_s, order, tmat)

        def mmat(i, jb, v):
            put(m_s, i, jb, t * at(m_s, i, jb) + v)

        symmetric(order, r_s, t_s, order, mmat)
        z = t * z
        if not last:

            def rmat(i, jb, v):
                if jb == i // size:
                    v = v + jnp.where(sub == i % size, z, 0.0)
                put(r_s, i, jb, v)
                put(q_s, i, jb, a_coef * at(m_s, i, jb) + v)

            symmetric(order, g_s, m_s, order, rmat)

    root = full(lax.rsqrt(scale))
    for i in range(order):
        for jb in range(nb):
            m_s[pl.ds(i * order + jb * size, size), :] = at(m_s, i, jb) * inv

    def cmat(l, carry):
        acc = [zero] * groups
        for k in range(order):
            lhs = row_of(m_s, l * order + k)
            for g in range(groups):
                acc[g] = acc[g] + lhs * bl_s[pl.ds(k * members + g * size, size), :]
        for g in range(groups):
            c_s[pl.ds(pl.multiple_of(l * members + g * size, size), size), :] = acc[g]
        return carry

    lax.fori_loop(0, order, cmat, 0)

    def smat_times(vector):
        for g in range(groups):
            t_s[pl.ds(g * size, size), :] = vector[g]
        down = [zero] * nb
        for k in range(members):
            v = row_of(t_s, k)
            for j in range(nb):
                down[j] = down[j] + v * bk_s[pl.ds(k * order + j * size, size), :]
        for j in range(nb):
            t_s[pl.ds(members + j * size, size), :] = down[j]
        up = [z * vector[g] for g in range(groups)]
        for l in range(order):
            u = row_of(t_s, members + l)
            for g in range(groups):
                up[g] = up[g] + u * c_s[pl.ds(l * members + g * size, size), :]
        return [root * up[g] for g in range(groups)]

    wbar = smat_times(smat_times(vec))
    for g in range(groups):
        t_s[pl.ds(g * size, size), :] = wbar[g]

    gain = full(jnp.float32(base) ** 0.5 * root)

    def vmat(k, carry):
        acc = [zero] * groups
        for l in range(order):
            lhs = row_of(bk_s, k * order + l)
            for g in range(groups):
                acc[g] = acc[g] + lhs * c_s[pl.ds(l * members + g * size, size), :]
        for g in range(groups):
            here = sub + g * size == k
            s = acc[g] + jnp.where(here, z, 0.0)
            v = gain * s + t_s[pl.ds(g * size, size), :] - jnp.where(here, 1.0, 0.0)
            v_s[pl.ds(pl.multiple_of(k * members + g * size, size), size), :] = v
        return carry

    lax.fori_loop(0, members, vmat, 0)

    half = members // 2

    def turn(k, carry):
        both = jnp.concatenate(
            [
                v_s[pl.ds(pl.multiple_of(k * members, members), members), :],
                v_s[pl.ds(pl.multiple_of((k + half) * members, members), members), :],
            ],
            axis=0,
        )
        w_s[pl.ds(pl.multiple_of(k * LANES, LANES), LANES), :] = jnp.transpose(both)
        return carry

    lax.fori_loop(0, half, turn, 0)

    def apply(pair, carry):
        region, place = pair // (size // 2), pair % (size // 2)
        start = pl.multiple_of(place * 2 * size, 2 * size)
        blocks = [
            ens_ref[g, region, pl.ds(start, 2 * size), :].astype(F32) for g in range(groups)
        ]
        outs = []
        for second in range(2):
            x = jnp.concatenate(
                [b[second * size : (second + 1) * size] for b in blocks], axis=0
            )
            x = (x - jnp.mean(x, axis=0, keepdims=True)).astype(BF16)
            gap = jnp.zeros_like(x)
            rhs = jnp.concatenate(
                [jnp.concatenate([x, gap], axis=1), jnp.concatenate([gap, x], axis=1)], axis=0
            )
            lhs = w_s[pl.ds(pair * 2 + second, half, stride=LANES), :].astype(BF16)
            outs.append(dot(lhs, rhs))
        for g in range(groups):
            top, side = g * size % half, g * size // half
            piece = [
                o[top : top + size, side * LANES : (side + 1) * LANES] for o in outs
            ]
            inc_ref[g, region, pl.ds(start, 2 * size), :] = jnp.concatenate(
                piece, axis=0
            ).astype(BF16)
        return carry

    lax.fori_loop(0, regions * size // 2, apply, 0, unroll=2)


def analyse(before, own, after, nbr, loc, ens):
    order, points = nbr.shape
    members = ens.shape[0] * 8
    panels = 3 * own.shape[1] // LANES
    small = pltpu.VMEM((order * order, LANES), F32)
    tall = pltpu.VMEM((order * members, LANES), F32)
    return pl.pallas_call(
        analyse_kernel,
        out_shape=jax.ShapeDtypeStruct(ens.shape, BF16),
        in_specs=[VM] * 6,
        out_specs=VM,
        scratch_shapes=[
            pltpu.VMEM((panels, members + 16, LANES), F32),
            tall,
            tall,
            small,
            small,
            small,
            small,
            small,
            tall,
            pltpu.VMEM((members * members, LANES), F32),
            pltpu.VMEM((members // 2 * LANES, LANES), F32),
        ],
        compiler_params=pltpu.CompilerParams(vmem_limit_bytes=56 * 2**20),
        name="analyse",
    )(before, own, after, nbr, loc, ens)


def finish_kernel(fore_ref, inc_ref, out_ref, sum_s):
    members, grid_r, _ = out_ref.shape
    tiles, rows, _ = fore_ref.shape

    def add(t, carry):
        sum_s[pl.ds(pl.multiple_of(t * rows, rows), rows), :] = fore_ref[t].astype(F32) + inc_ref[
            t
        ].astype(F32)
        return carry

    lax.fori_loop(0, tiles, add, 0, unroll=4)
    for k in range(members):
        out_ref[k] = sum_s[pl.ds(k, grid_r, stride=members), :].astype(BF16)


def finish(fore, inc, members):
    tiles, rows, _ = fore.shape
    grid_r = tiles * rows // members
    return pl.pallas_call(
        finish_kernel,
        out_shape=jax.ShapeDtypeStruct((members, grid_r, LANES), BF16),
        in_specs=[VM, VM],
        out_specs=VM,
        scratch_shapes=[pltpu.VMEM((tiles * rows, LANES), F32)],
        compiler_params=pltpu.CompilerParams(vmem_limit_bytes=40 * 2**20),
        name="finish",
    )(fore, inc)


def neighbours(last, first, axis, wrap):
    count = lax.axis_size(axis)
    up = [(i, (i + 1) % count) for i in range(count if wrap else count - 1)]
    down = [(j, i) for i, j in up]
    return lax.ppermute(last, axis, up), lax.ppermute(first, axis, down)


def exchange(blocks):
    return lax.all_to_all(blocks, MR, split_axis=0, concat_axis=0, tiled=True)


def shards(
    latent_vertex_values,
    background_field,
    edge_senders,
    grid_parent,
    w_send,
    w_recv,
    w_node,
    w_agg,
    w_out,
    norm_gain,
    w_dec,
    obs_loc,
    obs_count,
    obs_value,
    obs_var,
    obs_nbr,
    loc_weight,
):
    members = latent_vertex_values.shape[0]
    groups, regions = lax.axis_size("member"), lax.axis_size("region")
    before, after = neighbours(
        latent_vertex_values[:, -RIM:], latent_vertex_values[:, :RIM], "region", True
    )
    weights = (w_send, w_recv, w_node, w_agg, w_out, norm_gain[None], w_dec)
    processed, fore = forecast(
        latent_vertex_values, before, after, background_field, edge_senders, grid_parent, weights
    )
    ens = exchange(fore)
    ens = ens.reshape(groups, regions, *ens.shape[1:])
    payload = observe(ens, obs_loc, obs_count, obs_value, obs_var)
    pay_before, pay_after = neighbours(payload, payload, MR, False)
    inc = analyse(pay_before, payload, pay_after, obs_nbr, loc_weight, ens)
    landed = exchange(inc.reshape(groups * regions, *inc.shape[2:]))
    return processed, finish(fore, landed, members)


def solution(mesh):
    in_specs = (
        P("member", "region", None),
        P("member", "region", None),
        P("region", None),
        P("region"),
        P(),
        P(),
        P(),
        P(),
        P(),
        P(),
        P(),
        P(MR),
        P(MR),
        P(MR),
        P(MR),
        P(None, MR),
        P(None, MR),
    )
    out_specs = (P("member", "region", None), P("member", "region", None))
    return jax.shard_map(shards, mesh=mesh, in_specs=in_specs, out_specs=out_specs, check_vma=False)
```

```python
import functools

import jax
import jax.numpy as jnp
from jax import lax
from jax.experimental import pallas as pl
from jax.experimental.pallas import tpu as pltpu
from jax.sharding import PartitionSpec as P

NS_ITERS = 6
LANES = 128
RIM = 64
MEMBERS = 8
GROUP = 8
CHUNKS = 4
UNROLL = 8
F32 = jnp.float32
BF16 = jnp.bfloat16
MR = ("member", "region")
VM = pl.BlockSpec(memory_space=pltpu.VMEM)
SM = pl.BlockSpec(memory_space=pltpu.SMEM)


def dot(a, b):
    return jnp.dot(a, b, preferred_element_type=F32)


def forecast_kernel(
    edge_ref,
    parent_ref,
    latent_hbm,
    rim_ref,
    back_hbm,
    w_send_ref,
    w_recv_ref,
    w_node_hbm,
    w_agg_hbm,
    w_out_hbm,
    gain_ref,
    w_dec_hbm,
    proc_hbm,
    fore_hbm,
    send_s,
    recv_s,
    dec_s,
    latent_s,
    back_s,
    proc_s,
    fore_s,
    w_node_s,
    w_agg_s,
    w_out_s,
    w_dec_s,
    in_sem,
    out_sem,
):
    members = MEMBERS
    count, width = latent_hbm.shape
    nodes = count // members
    rim = rim_ref.shape[0] // 2
    degree = edge_ref.shape[0] // nodes
    rows = count // CHUNKS
    tile = members * GROUP

    def piece(c):
        return pl.ds(pl.multiple_of(c * rows, rows), rows)

    loads = [
        pltpu.make_async_copy(latent_hbm.at[piece(c)], latent_s.at[piece(c)], in_sem.at[c])
        for c in range(CHUNKS)
    ]
    later = [
        pltpu.make_async_copy(src, dst, in_sem.at[CHUNKS + i])
        for i, (src, dst) in enumerate(
            [
                (w_node_hbm, w_node_s),
                (w_agg_hbm, w_agg_s),
                (w_out_hbm, w_out_s),
                (w_dec_hbm, w_dec_s),
                (back_hbm, back_s),
            ]
        )
    ]
    for copy in loads + later:
        copy.start()

    def send_of(state):
        return dot(state, w_send_ref[...]).astype(BF16).astype(F32) * 0.5

    cols = width // LANES

    def spread_rows(ref, first, values):
        for c in range(cols):
            part = values[:, c * LANES : (c + 1) * LANES].reshape(-1, members, LANES)
            ref[first // members : first // members + part.shape[0], c] = part

    spread_rows(send_s, 0, send_of(rim_ref[0:rim]))
    spread_rows(send_s, rim + count, send_of(rim_ref[rim : 2 * rim]))
    for c in range(CHUNKS):
        loads[c].wait()
        state = latent_s[c * rows : (c + 1) * rows]
        spread_rows(send_s, rim + c * rows, send_of(state))
        spread_rows(recv_s, c * rows, dot(state, w_recv_ref[...]) * 0.5)

    def aggregate(n, carry):
        mine = recv_s[n]
        total = jnp.zeros_like(mine)
        for e in range(degree):
            half = send_s[edge_ref[n * degree + e]] + mine
            total = total + (half + half * jnp.tanh(half))
        recv_s[n] = total
        return carry

    lax.fori_loop(0, nodes, aggregate, 0, unroll=8)
    for copy in later:
        copy.wait()

    def store_proc(c):
        return pltpu.make_async_copy(proc_s.at[piece(c)], proc_hbm.at[piece(c)], out_sem.at[c])

    def update(c, carry):
        state = latent_s[piece(c)]
        some_nodes = pl.ds(c * (rows // members), rows // members)
        agg = jnp.concatenate(
            [recv_s[some_nodes, i].reshape(rows, LANES) for i in range(cols)], axis=1
        ).astype(BF16)
        pre = (dot(state, w_node_s[...]) + dot(agg, w_agg_s[...])) * 0.5
        hidden = (pre + pre * jnp.tanh(pre)).astype(BF16)
        out = dot(hidden, w_out_s[...])
        mean = jnp.mean(out, axis=-1, keepdims=True)
        centred = out - mean
        var = jnp.mean(centred * centred, axis=-1, keepdims=True)
        norm = centred * lax.rsqrt(var + 1e-05) * gain_ref[...]
        proc = (state.astype(F32) + norm).astype(BF16)
        proc_s[piece(c)] = proc
        store_proc(c).start()
        dec_s[piece(c)] = dot(proc, w_dec_s[...])
        return carry

    lax.fori_loop(0, CHUNKS, update, 0)

    tiles = fore_s.shape[0]
    some = tiles // CHUNKS

    def store_fore(c):
        span = pl.ds(c * some, some)
        return pltpu.make_async_copy(fore_s.at[span], fore_hbm.at[span], out_sem.at[CHUNKS + c])

    for c in range(CHUNKS):

        def spread(t, carry):
            parts = [
                dec_s[pl.ds(pl.multiple_of(parent_ref[t * GROUP + q], members), members), :]
                for q in range(GROUP)
            ]
            back = back_s[pl.ds(pl.multiple_of(t * tile, tile), tile), :].astype(F32)
            fore_s[t] = (jnp.concatenate(parts, axis=0) + back).astype(BF16)
            return carry

        lax.fori_loop(c * some, (c + 1) * some, spread, 0, unroll=4)
        store_fore(c).start()

    for c in range(CHUNKS):
        store_proc(c).wait()
        store_fore(c).wait()


def forecast(latent, rims, back, senders, parent, weights):
    count, width = latent.shape
    grid_rows = back.shape[0]
    rim = rims.shape[0] // 2
    tiles = lax.axis_size("member") * lax.axis_size("region")
    edge = (senders - (count - rim) // MEMBERS).reshape(-1)
    hbm = pl.BlockSpec(memory_space=pl.ANY)
    w_shape = pltpu.VMEM(weights[2].shape, BF16)
    return pl.pallas_call(
        forecast_kernel,
        out_shape=(
            jax.ShapeDtypeStruct(latent.shape, BF16),
            jax.ShapeDtypeStruct((tiles, grid_rows // tiles, LANES), BF16),
        ),
        in_specs=[SM, SM, hbm, VM, hbm, VM, VM, hbm, hbm, hbm, VM, hbm],
        out_specs=(hbm, hbm),
        scratch_shapes=[
            pltpu.VMEM(((count + 2 * rim) // MEMBERS, width // LANES, MEMBERS, LANES), F32),
            pltpu.VMEM((count // MEMBERS, width // LANES, MEMBERS, LANES), F32),
            pltpu.VMEM((count, LANES), F32),
            pltpu.VMEM(latent.shape, BF16),
            pltpu.VMEM(back.shape, BF16),
            pltpu.VMEM(latent.shape, BF16),
            pltpu.VMEM((tiles, grid_rows // tiles, LANES), BF16),
            w_shape,
            w_shape,
            w_shape,
            pltpu.VMEM(weights[6].shape, BF16),
            pltpu.SemaphoreType.DMA((CHUNKS + 5,)),
            pltpu.SemaphoreType.DMA((2 * CHUNKS,)),
        ],
        compiler_params=pltpu.CompilerParams(vmem_limit_bytes=56 * 2**20),
        name="forecast",
    )(edge, parent * MEMBERS, latent, rims, back, *weights)


def observe_kernel(loc_ref, count_ref, ens_ref, value_ref, var_ref, pay_ref):
    groups, regions, rows, _ = ens_ref.shape
    size = 8
    members = groups * size
    slots = loc_ref.shape[0]
    lane = lax.broadcasted_iota(jnp.int32, (members, LANES), 1)
    for part in range(slots // LANES):

        def take(i, acc):
            loc = loc_ref[part * LANES + i]
            point, channel = loc % LANES, loc // LANES
            region, place = point // size, point % size
            start = pl.multiple_of(place // 2 * 2 * size, 2 * size)
            second = place % 2
            pieces = []
            for g in range(groups):
                pair = ens_ref[g, region, pl.ds(start, 2 * size), :].astype(F32)
                pieces.append(jnp.where(second == 1, pair[size:], pair[:size]))
            block = jnp.concatenate(pieces, axis=0)
            turned = pltpu.roll(block, (i - channel + LANES) % LANES, 1)
            return jnp.where(lane == i, turned, acc)

        yens = lax.fori_loop(0, LANES, take, jnp.zeros((members, LANES), F32), unroll=8)
        span = slice(part * LANES, (part + 1) * LANES)
        ybar = jnp.mean(yens, axis=0, keepdims=True)
        slot = lax.broadcasted_iota(jnp.int32, (1, LANES), 1) + part * LANES
        rinv = jnp.where(slot < count_ref[0], 1.0, 0.0) / var_ref[:, span]
        dres = (value_ref[:, span] - ybar) * rinv
        row = lax.broadcasted_iota(jnp.int32, (16, LANES), 0)
        extra = jnp.where(row == 0, rinv, jnp.where(row == 1, dres, 0.0))
        pay_ref[0:members, span] = (yens - ybar).astype(BF16)
        pay_ref[members : members + 16, span] = extra.astype(BF16)


def observe(ens, loc, count, value, var):
    groups, regions, rows, _ = ens.shape
    return pl.pallas_call(
        observe_kernel,
        out_shape=jax.ShapeDtypeStruct((groups * 8 + 16, loc.shape[0]), BF16),
        in_specs=[SM, SM, VM, VM, VM],
        out_specs=VM,
        compiler_params=pltpu.CompilerParams(vmem_limit_bytes=40 * 2**20),
        name="observe",
    )(loc, count, ens, value[None], var[None])


def analyse_kernel(
    before_ref,
    own_ref,
    after_ref,
    nbr_ref,
    loc_ref,
    ens_ref,
    inc_ref,
    pay_s,
    bl_s,
    bk_s,
    g_s,
    m_s,
    r_s,
    q_s,
    t_s,
    c_s,
    v_s,
    w_s,
):
    groups, regions, rows, _ = ens_ref.shape
    size = 8
    members = groups * size
    order = nbr_ref.shape[0]
    nb = order // size
    slots = own_ref.shape[1]
    parts = slots // LANES
    sub = lax.broadcasted_iota(jnp.int32, (size, LANES), 0)

    for i, ref in enumerate((before_ref, own_ref, after_ref)):
        for h in range(parts):
            pay_s[i * parts + h] = ref[0 : members + 16, h * LANES : (h + 1) * LANES].astype(F32)

    def full(row):
        return jnp.broadcast_to(row, (size, LANES))

    def gather(l, vec):
        index = nbr_ref[pl.ds(l, 1), :]
        lane = full(index % LANES)
        panel = full(index // LANES)
        masks = [panel == j for j in range(1, 3 * parts)]

        def pick(first):
            out = None
            for j in range(3 * parts):
                got = jnp.take_along_axis(
                    pay_s[j, pl.ds(first, size), :], lane, axis=1, mode="promise_in_bounds"
                )
                out = got if out is None else jnp.where(masks[j - 1], got, out)
            return out

        extra = pick(members)
        weight = loc_ref[pl.ds(l, 1), :]
        root = jnp.sqrt(weight * extra[0:1])
        dl = weight * extra[1:2]
        new = []
        for g in range(groups):
            yl = pick(g * size)
            new.append(vec[g] + yl * dl)
            b = yl * root
            bl_s[pl.ds(pl.multiple_of(l * members + g * size, size), size), :] = b
            bk_s[pl.ds(g * size * order + l, size, stride=order), :] = b
        return tuple(new)

    zero = jnp.zeros((size, LANES), F32)
    vec = lax.fori_loop(0, order, gather, tuple([zero] * groups), unroll=2)

    def row_of(ref, r):
        return jnp.broadcast_to(ref[pl.ds(r, 1), :], (size, LANES))

    def accumulate(start, stop, left_row, right, a, acc):
        width = nb - a

        def body(k, acc):
            rhs = [
                right[pl.ds(pl.multiple_of(k * order + (a + j) * size, size), size), :]
                for j in range(width)
            ]
            out = []
            for i in range(size):
                lhs = left_row(k, i)
                for j in range(width):
                    out.append(acc[i * width + j] + lhs * rhs[j])
            return tuple(out)

        return lax.fori_loop(start, stop, body, acc, unroll=UNROLL)

    def finish_group(a, acc, finish):
        width = nb - a
        for i in range(size):
            for j in range(width):
                finish(a * size + i, a + j, acc[i * width + j])

    def gram(ref, count, finish):
        for a in range(nb):
            acc = accumulate(
                0,
                count,
                lambda k, i: row_of(ref, k * order + a * size + i),
                ref,
                a,
                tuple([zero] * (size * (nb - a))),
            )
            finish_group(a, acc, finish)

    def product(left, right, finish):
        for a in range(nb):
            edge = (a + 1) * size
            acc = accumulate(
                0,
                edge,
                lambda k, i: row_of(left, k * order + a * size + i),
                right,
                a,
                tuple([zero] * (size * (nb - a))),
            )
            if edge < order:
                acc = accumulate(
                    edge,
                    order,
                    lambda k, i: row_of(left, (a * size + i) * order + k),
                    right,
                    a,
                    acc,
                )
            finish_group(a, acc, finish)

    def at(ref, i, jb):
        return ref[pl.ds(i * order + jb * size, size), :]

    def put(ref, i, jb, value):
        ref[pl.ds(i * order + jb * size, size), :] = value
        if jb != i // size:
            ref[pl.ds(jb * size * order + i, size, stride=order), :] = value

    def upper(ref, i, jb, value):
        ref[pl.ds(i * order + jb * size, size), :] = value

    blocks = [(i, jb) for i in range(order) for jb in range(i // size, nb)]
    gram(bk_s, members, functools.partial(upper, g_s))

    square, cross, trace = zero, zero, zero
    for i, jb in blocks:
        g = at(g_s, i, jb)
        if jb == i // size:
            square = square + g * g
            trace = trace + jnp.where(sub == i % size, g, 0.0)
        else:
            cross = cross + g * g
    square = square + 2.0 * cross
    base = members - 1.0
    total = (
        base * base * members
        + 2.0 * base * jnp.sum(trace, axis=0, keepdims=True)
        + jnp.sum(square, axis=0, keepdims=True)
    )
    scale = jnp.sqrt(total)
    inv = 1.0 / scale
    a_coef = full(base * inv)

    z = 1.5 - 0.5 * a_coef
    for i, jb in blocks:
        g = at(g_s, i, jb) * inv
        put(g_s, i, jb, g)
        m, r = zero, -0.5 * g
        if jb == i // size:
            here = sub == i % size
            m = jnp.where(here, -0.5, 0.0)
            r = r + jnp.where(here, z, 0.0)
        upper(m_s, i, jb, m)
        put(r_s, i, jb, r)
        upper(q_s, i, jb, a_coef * m + r)

    for it in range(1, NS_ITERS):
        last = it == NS_ITERS - 1
        t = 1.5 - 0.5 * a_coef * z * z

        def tmat(i, jb, v):
            upper(t_s, i, jb, -0.5 * (v + z * (at(q_s, i, jb) - at(r_s, i, jb))))

        product(q_s, r_s, tmat)

        def mmat(i, jb, v):
            m = t * at(m_s, i, jb) + v
            if last:
                put(m_s, i, jb, m * inv)
            else:
                upper(m_s, i, jb, m)

        product(t_s, r_s, mmat)
        z = t * z
        if not last:

            def rmat(i, jb, v):
                if jb == i // size:
                    v = v + jnp.where(sub == i % size, z, 0.0)
                put(r_s, i, jb, v)
                upper(q_s, i, jb, a_coef * at(m_s, i, jb) + v)

            product(m_s, g_s, rmat)

    root = full(lax.rsqrt(scale))

    def cmat(step, carry):
        for g0 in range(0, groups, 4):
            acc = [zero] * 16
            for k in range(order):
                b = [bl_s[pl.ds(k * members + (g0 + g) * size, size), :] for g in range(4)]
                for i in range(4):
                    lhs = row_of(m_s, k * order + step * 4 + i)
                    for g in range(4):
                        acc[i * 4 + g] = acc[i * 4 + g] + lhs * b[g]
            for i in range(4):
                for g in range(4):
                    start = (step * 4 + i) * members + (g0 + g) * size
                    c_s[pl.ds(pl.multiple_of(start, size), size), :] = acc[i * 4 + g]
        return carry

    lax.fori_loop(0, order // 4, cmat, 0)

    def smat_times(vector):
        for g in range(groups):
            t_s[pl.ds(g * size, size), :] = vector[g]
        down = [zero] * nb
        for k in range(members):
            v = row_of(t_s, k)
            for j in range(nb):
                down[j] = down[j] + v * bk_s[pl.ds(k * order + j * size, size), :]
        for j in range(nb):
            t_s[pl.ds(members + j * size, size), :] = down[j]
        up = [z * vector[g] for g in range(groups)]
        for l in range(order):
            u = row_of(t_s, members + l)
            for g in range(groups):
                up[g] = up[g] + u * c_s[pl.ds(l * members + g * size, size), :]
        return [root * up[g] for g in range(groups)]

    wbar = smat_times(smat_times(vec))
    for g in range(groups):
        t_s[pl.ds(g * size, size), :] = wbar[g]

    gain = full(jnp.float32(base) ** 0.5 * root)

    def vmat(step, carry):
        for g0 in range(0, groups, 4):
            acc = [zero] * 16
            for l in range(order):
                c = [c_s[pl.ds(l * members + (g0 + g) * size, size), :] for g in range(4)]
                for i in range(4):
                    lhs = row_of(bk_s, (step * 4 + i) * order + l)
                    for g in range(4):
                        acc[i * 4 + g] = acc[i * 4 + g] + lhs * c[g]
            for i in range(4):
                k = step * 4 + i
                for g in range(4):
                    here = sub + (g0 + g) * size == k
                    s = gain * (acc[i * 4 + g] + jnp.where(here, z, 0.0))
                    v = s + t_s[pl.ds((g0 + g) * size, size), :] - jnp.where(here, 1.0, 0.0)
                    start = k * members + (g0 + g) * size
                    v_s[pl.ds(pl.multiple_of(start, size), size), :] = v
        return carry

    lax.fori_loop(0, members // 4, vmat, 0)

    half = members // 2

    def turn(k, carry):
        both = jnp.concatenate(
            [
                v_s[pl.ds(pl.multiple_of(k * members, members), members), :],
                v_s[pl.ds(pl.multiple_of((k + half) * members, members), members), :],
            ],
            axis=0,
        )
        w_s[pl.ds(pl.multiple_of(k * LANES, LANES), LANES), :] = jnp.transpose(both)
        return carry

    lax.fori_loop(0, half, turn, 0)

    def apply(pair, carry):
        region, place = pair // (size // 2), pair % (size // 2)
        start = pl.multiple_of(place * 2 * size, 2 * size)
        blocks = [
            ens_ref[g, region, pl.ds(start, 2 * size), :].astype(F32) for g in range(groups)
        ]
        outs = []
        for second in range(2):
            x = jnp.concatenate(
                [b[second * size : (second + 1) * size] for b in blocks], axis=0
            )
            x = (x - jnp.mean(x, axis=0, keepdims=True)).astype(BF16)
            gap = jnp.zeros_like(x)
            rhs = jnp.concatenate(
                [jnp.concatenate([x, gap], axis=1), jnp.concatenate([gap, x], axis=1)], axis=0
            )
            lhs = w_s[pl.ds(pair * 2 + second, half, stride=LANES), :].astype(BF16)
            outs.append(dot(lhs, rhs))
        for g in range(groups):
            top, side = g * size % half, g * size // half
            piece = [
                o[top : top + size, side * LANES : (side + 1) * LANES] for o in outs
            ]
            inc_ref[g, region, pl.ds(start, 2 * size), :] = jnp.concatenate(
                piece, axis=0
            ).astype(BF16)
        return carry

    lax.fori_loop(0, regions * size // 2, apply, 0, unroll=8)


def analyse(before, own, after, nbr, loc, ens):
    order, points = nbr.shape
    members = ens.shape[0] * 8
    panels = 3 * own.shape[1] // LANES
    small = pltpu.VMEM((order * order, LANES), F32)
    tall = pltpu.VMEM((order * members, LANES), F32)
    return pl.pallas_call(
        analyse_kernel,
        out_shape=jax.ShapeDtypeStruct(ens.shape, BF16),
        in_specs=[VM] * 6,
        out_specs=VM,
        scratch_shapes=[
            pltpu.VMEM((panels, members + 16, LANES), F32),
            tall,
            tall,
            small,
            small,
            small,
            small,
            small,
            tall,
            pltpu.VMEM((members * members, LANES), F32),
            pltpu.VMEM((members // 2 * LANES, LANES), F32),
        ],
        compiler_params=pltpu.CompilerParams(vmem_limit_bytes=56 * 2**20),
        name="analyse",
    )(before, own, after, nbr, loc, ens)


def finish_kernel(fore_ref, inc_ref, out_ref, sum_s):
    members, grid_r, _ = out_ref.shape
    tiles, rows, _ = fore_ref.shape

    def add(t, carry):
        sum_s[pl.ds(pl.multiple_of(t * rows, rows), rows), :] = fore_ref[t].astype(F32) + inc_ref[
            t
        ].astype(F32)
        return carry

    lax.fori_loop(0, tiles, add, 0, unroll=4)
    for k in range(members):
        out_ref[k] = sum_s[pl.ds(k, grid_r, stride=members), :].astype(BF16)


def finish(fore, inc, members):
    tiles, rows, _ = fore.shape
    grid_r = tiles * rows // members
    return pl.pallas_call(
        finish_kernel,
        out_shape=jax.ShapeDtypeStruct((members, grid_r, LANES), BF16),
        in_specs=[VM, VM],
        out_specs=VM,
        scratch_shapes=[pltpu.VMEM((tiles * rows, LANES), F32)],
        compiler_params=pltpu.CompilerParams(vmem_limit_bytes=40 * 2**20),
        name="finish",
    )(fore, inc)


def neighbours(last, first, axis, wrap):
    count = lax.axis_size(axis)
    up = [(i, (i + 1) % count) for i in range(count if wrap else count - 1)]
    down = [(j, i) for i, j in up]
    return lax.ppermute(last, axis, up), lax.ppermute(first, axis, down)


def exchange(blocks):
    return lax.all_to_all(blocks, MR, split_axis=0, concat_axis=0, tiled=True)


def shards(
    latent_vertex_values,
    background_field,
    edge_senders,
    grid_parent,
    w_send,
    w_recv,
    w_node,
    w_agg,
    w_out,
    norm_gain,
    w_dec,
    obs_loc,
    obs_count,
    obs_value,
    obs_var,
    obs_nbr,
    loc_weight,
):
    members, nodes, width = latent_vertex_values.shape
    grid_r = background_field.shape[1]
    groups, regions = lax.axis_size("member"), lax.axis_size("region")

    def node_major(array):
        return array.transpose(1, 0, 2).reshape(-1, array.shape[2])

    before, after = neighbours(
        node_major(latent_vertex_values[:, -RIM:]),
        node_major(latent_vertex_values[:, :RIM]),
        "region",
        True,
    )
    weights = (w_send, w_recv, w_node, w_agg, w_out, norm_gain[None], w_dec)
    processed, fore = forecast(
        node_major(latent_vertex_values),
        jnp.concatenate([before, after], axis=0),
        node_major(background_field),
        edge_senders,
        grid_parent,
        weights,
    )
    processed = processed.reshape(nodes, members, width).transpose(1, 0, 2)
    ens = exchange(fore)
    ens = ens.reshape(groups, regions, *ens.shape[1:])
    payload = observe(ens, obs_loc, obs_count, obs_value, obs_var)
    pay_before, pay_after = neighbours(payload, payload, MR, False)
    inc = analyse(pay_before, payload, pay_after, obs_nbr, loc_weight, ens)
    landed = exchange(inc.reshape(groups * regions, *inc.shape[2:]))
    return processed, finish(fore, landed, members)


def solution(mesh):
    in_specs = (
        P("member", "region", None),
        P("member", "region", None),
        P("region", None),
        P("region"),
        P(),
        P(),
        P(),
        P(),
        P(),
        P(),
        P(),
        P(MR),
        P(MR),
        P(MR),
        P(MR),
        P(None, MR),
        P(None, MR),
    )
    out_specs = (P("member", "region", None), P("member", "region", None))
    return jax.shard_map(shards, mesh=mesh, in_specs=in_specs, out_specs=out_specs, check_vma=False)
```

```python
import functools

import jax
import jax.numpy as jnp
from jax import lax
from jax.experimental import pallas as pl
from jax.experimental.pallas import tpu as pltpu
from jax.sharding import PartitionSpec as P

NS_ITERS = 6
LANES = 128
RIM = 64
MEMBERS = 8
GROUP = 8
CHUNKS = 4
UNROLL = 8
F32 = jnp.float32
BF16 = jnp.bfloat16
MR = ("member", "region")
VM = pl.BlockSpec(memory_space=pltpu.VMEM)
SM = pl.BlockSpec(memory_space=pltpu.SMEM)


def dot(a, b):
    return jnp.dot(a, b, preferred_element_type=F32)


def forecast_kernel(
    edge_ref,
    parent_ref,
    latent_hbm,
    before_ref,
    after_ref,
    back_hbm,
    w_send_ref,
    w_recv_ref,
    w_node_hbm,
    w_agg_hbm,
    w_out_hbm,
    gain_ref,
    w_dec_hbm,
    proc_hbm,
    fore_hbm,
    send_s,
    recv_s,
    dec_s,
    latent_s,
    back_s,
    proc_s,
    fore_s,
    w_node_s,
    w_agg_s,
    w_out_s,
    w_dec_s,
    in_sem,
    out_sem,
):
    members = MEMBERS
    count, width = latent_hbm.shape
    nodes = count // members
    rim = before_ref.shape[0]
    degree = edge_ref.shape[0] // nodes
    rows = count // CHUNKS
    tile = members * GROUP

    def piece(c):
        return pl.ds(c * rows, rows)

    loads = [
        pltpu.make_async_copy(latent_hbm.at[piece(c)], latent_s.at[piece(c)], in_sem.at[c])
        for c in range(CHUNKS)
    ]
    later = [
        pltpu.make_async_copy(src, dst, in_sem.at[CHUNKS + i])
        for i, (src, dst) in enumerate(
            [
                (w_node_hbm, w_node_s),
                (w_agg_hbm, w_agg_s),
                (w_out_hbm, w_out_s),
                (w_dec_hbm, w_dec_s),
                (back_hbm, back_s),
            ]
        )
    ]
    for copy in loads + later:
        copy.start()

    def send_of(state):
        return dot(state, w_send_ref[...]).astype(BF16).astype(F32) * 0.5

    cols = width // LANES

    def spread_rows(ref, first, values):
        for c in range(cols):
            part = values[:, c * LANES : (c + 1) * LANES].reshape(-1, members, LANES)
            ref[first // members : first // members + part.shape[0], c] = part

    spread_rows(send_s, 0, send_of(before_ref[...]))
    spread_rows(send_s, rim + count, send_of(after_ref[...]))
    for c in range(CHUNKS):
        loads[c].wait()
        state = latent_s[c * rows : (c + 1) * rows]
        spread_rows(send_s, rim + c * rows, send_of(state))
        spread_rows(recv_s, c * rows, dot(state, w_recv_ref[...]) * 0.5)

    def aggregate(n, carry):
        mine = recv_s[n]
        total = jnp.zeros_like(mine)
        for e in range(degree):
            half = send_s[edge_ref[n * degree + e]] + mine
            total = total + (half + half * jnp.tanh(half))
        recv_s[n] = total
        return carry

    lax.fori_loop(0, nodes, aggregate, 0, unroll=8)
    for copy in later:
        copy.wait()

    def store_proc(c):
        return pltpu.make_async_copy(proc_s.at[piece(c)], proc_hbm.at[piece(c)], out_sem.at[c])

    def update(c):
        state = latent_s[piece(c)]
        some_nodes = pl.ds(c * (rows // members), rows // members)
        agg = jnp.concatenate(
            [recv_s[some_nodes, i].reshape(rows, LANES) for i in range(cols)], axis=1
        ).astype(BF16)
        pre = (dot(state, w_node_s[...]) + dot(agg, w_agg_s[...])) * 0.5
        hidden = (pre + pre * jnp.tanh(pre)).astype(BF16)
        out = dot(hidden, w_out_s[...])
        mean = jnp.mean(out, axis=-1, keepdims=True)
        centred = out - mean
        var = jnp.mean(centred * centred, axis=-1, keepdims=True)
        norm = centred * lax.rsqrt(var + 1e-05) * gain_ref[...]
        proc = (state.astype(F32) + norm).astype(BF16)
        proc_s[piece(c)] = proc
        store_proc(c).start()
        dec_s[some_nodes] = dot(proc, w_dec_s[...]).reshape(-1, members, LANES)

    for c in range(CHUNKS):
        update(c)

    tiles = fore_s.shape[0]
    some = tiles // CHUNKS

    def store_fore(c):
        span = pl.ds(c * some, some)
        return pltpu.make_async_copy(fore_s.at[span], fore_hbm.at[span], out_sem.at[CHUNKS + c])

    for c in range(CHUNKS):

        def spread(t, carry):
            parts = [
                dec_s[parent_ref[t * GROUP + q]] for q in range(GROUP)
            ]
            back = back_s[pl.ds(pl.multiple_of(t * tile, tile), tile), :].astype(F32)
            fore_s[t] = (jnp.concatenate(parts, axis=0) + back).astype(BF16)
            return carry

        lax.fori_loop(c * some, (c + 1) * some, spread, 0, unroll=4)
        store_fore(c).start()

    for c in range(CHUNKS):
        store_proc(c).wait()
        store_fore(c).wait()


def forecast(latent, before, after, back, senders, parent, weights):
    count, width = latent.shape
    grid_rows = back.shape[0]
    rim = before.shape[0]
    tiles = lax.axis_size("member") * lax.axis_size("region")
    hbm = pl.BlockSpec(memory_space=pl.ANY)
    w_shape = pltpu.VMEM(weights[2].shape, BF16)
    return pl.pallas_call(
        forecast_kernel,
        out_shape=(
            jax.ShapeDtypeStruct(latent.shape, BF16),
            jax.ShapeDtypeStruct((tiles, grid_rows // tiles, LANES), BF16),
        ),
        in_specs=[SM, SM, hbm, VM, VM, hbm, VM, VM, hbm, hbm, hbm, VM, hbm],
        out_specs=(hbm, hbm),
        scratch_shapes=[
            pltpu.VMEM(((count + 2 * rim) // MEMBERS, width // LANES, MEMBERS, LANES), F32),
            pltpu.VMEM((count // MEMBERS, width // LANES, MEMBERS, LANES), F32),
            pltpu.VMEM((count // MEMBERS, MEMBERS, LANES), F32),
            pltpu.VMEM(latent.shape, BF16),
            pltpu.VMEM(back.shape, BF16),
            pltpu.VMEM(latent.shape, BF16),
            pltpu.VMEM((tiles, grid_rows // tiles, LANES), BF16),
            w_shape,
            w_shape,
            w_shape,
            pltpu.VMEM(weights[6].shape, BF16),
            pltpu.SemaphoreType.DMA((CHUNKS + 5,)),
            pltpu.SemaphoreType.DMA((2 * CHUNKS,)),
        ],
        compiler_params=pltpu.CompilerParams(vmem_limit_bytes=56 * 2**20),
        name="forecast",
    )(senders.reshape(-1), parent, latent, before, after, back, *weights)


def point_rows(ens_ref, region, start):
    size = 8
    blocks = [
        ens_ref[g, region, pl.ds(start, 2 * size), :].astype(F32) for g in range(ens_ref.shape[0])
    ]
    return [
        jnp.concatenate([b[i * size : (i + 1) * size] for b in blocks], axis=0) for i in range(2)
    ]


def observe_kernel(count_ref, loc_ref, ens_ref, value_ref, var_ref, pay_ref):
    groups, regions, rows, _ = ens_ref.shape
    size = 8
    members = groups * size
    slots = loc_ref.shape[1]
    pairs = size // 2
    loc = loc_ref[...]
    flat = loc % LANES * LANES + loc // LANES
    entry = lax.broadcasted_iota(jnp.int32, (2 * LANES, slots), 0)

    def add(pair, acc):
        start = pl.multiple_of(pair % pairs * 2 * size, 2 * size)
        state = jnp.concatenate(point_rows(ens_ref, pair // pairs, start), axis=1).astype(BF16)
        chosen = jnp.where(entry == flat - pair * 2 * LANES, 1.0, 0.0).astype(BF16)
        return acc + dot(state, chosen)

    yens = lax.fori_loop(0, regions * pairs, add, jnp.zeros((members, slots), F32), unroll=8)
    ybar = jnp.mean(yens, axis=0, keepdims=True)
    slot = lax.broadcasted_iota(jnp.int32, (1, slots), 1)
    rinv = jnp.where(slot < count_ref[0], 1.0, 0.0) / var_ref[...]
    dres = (value_ref[...] - ybar) * rinv
    row = lax.broadcasted_iota(jnp.int32, (16, slots), 0)
    extra = jnp.where(row == 0, rinv, jnp.where(row == 1, dres, 0.0))
    pay_ref[0:members] = (yens - ybar).astype(BF16)
    pay_ref[members : members + 16] = extra.astype(BF16)


def observe(ens, loc, count, value, var):
    groups, regions, rows, _ = ens.shape
    return pl.pallas_call(
        observe_kernel,
        out_shape=jax.ShapeDtypeStruct((groups * 8 + 16, loc.shape[0]), BF16),
        in_specs=[SM, VM, VM, VM, VM],
        out_specs=VM,
        compiler_params=pltpu.CompilerParams(vmem_limit_bytes=40 * 2**20),
        name="observe",
    )(count, loc[None], ens, value[None], var[None])


def analyse_kernel(
    before_ref,
    own_ref,
    after_ref,
    nbr_ref,
    loc_ref,
    ens_hbm,
    inc_hbm,
    ens_ref,
    inc_ref,
    pay_s,
    bl_s,
    bk_s,
    g_s,
    m_s,
    r_s,
    q_s,
    t_s,
    c_s,
    w_s,
    in_sem,
    out_sem,
):
    groups, regions, rows, _ = ens_ref.shape
    load = pltpu.make_async_copy(ens_hbm, ens_ref, in_sem.at[0])
    load.start()
    size = 8
    members = groups * size
    order = nbr_ref.shape[0]
    nb = order // size
    slots = own_ref.shape[1]
    sub = lax.broadcasted_iota(jnp.int32, (size, LANES), 0)

    for i, ref in enumerate((before_ref, own_ref, after_ref)):
        pay_s[:, i * slots : (i + 1) * slots] = ref[...]

    def full(row):
        return jnp.broadcast_to(row, (size, LANES))

    entry = lax.broadcasted_iota(jnp.int32, (3 * slots, 2 * LANES), 0)

    def gather(step, vec):
        index = jnp.concatenate(
            [nbr_ref[pl.ds(2 * step, 1), :], nbr_ref[pl.ds(2 * step + 1, 1), :]], axis=1
        )
        chosen = jnp.where(entry == index, 1.0, 0.0).astype(BF16)
        both = dot(pay_s[...], chosen)
        vec = list(vec)
        for i in range(2):
            l = 2 * step + i
            panel = both[:, i * LANES : (i + 1) * LANES]
            weight = loc_ref[pl.ds(l, 1), :]
            root = jnp.sqrt(weight * panel[members : members + 1])
            dl = weight * panel[members + 1 : members + 2]
            for g in range(groups):
                yl = panel[g * size : (g + 1) * size]
                vec[g] = vec[g] + yl * dl
                b = yl * root
                bl_s[pl.ds(pl.multiple_of(l * members + g * size, size), size), :] = b
                bk_s[pl.ds(g * size * order + l, size, stride=order), :] = b
        return tuple(vec)

    zero = jnp.zeros((size, LANES), F32)
    vec = lax.fori_loop(0, order // 2, gather, tuple([zero] * groups), unroll=2)

    def row_of(ref, r):
        return jnp.broadcast_to(ref[pl.ds(r, 1), :], (size, LANES))

    def accumulate(start, stop, left_row, right, a, acc):
        width = nb - a

        def body(k, acc):
            rhs = [
                right[pl.ds(pl.multiple_of(k * order + (a + j) * size, size), size), :]
                for j in range(width)
            ]
            out = []
            for i in range(size):
                lhs = left_row(k, i)
                for j in range(width):
                    out.append(acc[i * width + j] + lhs * rhs[j])
            return tuple(out)

        return lax.fori_loop(start, stop, body, acc, unroll=UNROLL)

    def finish_group(a, acc, finish):
        width = nb - a
        for i in range(size):
            for j in range(width):
                finish(a * size + i, a + j, acc[i * width + j])

    def gram(ref, count, finish):
        for a in range(nb):
            acc = accumulate(
                0,
                count,
                lambda k, i: row_of(ref, k * order + a * size + i),
                ref,
                a,
                tuple([zero] * (size * (nb - a))),
            )
            finish_group(a, acc, finish)

    def product(left, right, finish):
        for a in range(nb):
            edge = (a + 1) * size
            acc = accumulate(
                0,
                edge,
                lambda k, i: row_of(left, k * order + a * size + i),
                right,
                a,
                tuple([zero] * (size * (nb - a))),
            )
            if edge < order:
                acc = accumulate(
                    edge,
                    order,
                    lambda k, i: row_of(left, (a * size + i) * order + k),
                    right,
                    a,
                    acc,
                )
            finish_group(a, acc, finish)

    def at(ref, i, jb):
        return ref[pl.ds(i * order + jb * size, size), :]

    def put(ref, i, jb, value):
        ref[pl.ds(i * order + jb * size, size), :] = value
        if jb != i // size:
            ref[pl.ds(jb * size * order + i, size, stride=order), :] = value

    def upper(ref, i, jb, value):
        ref[pl.ds(i * order + jb * size, size), :] = value

    blocks = [(i, jb) for i in range(order) for jb in range(i // size, nb)]
    gram(bk_s, members, functools.partial(upper, g_s))

    square, cross, trace = zero, zero, zero
    for i, jb in blocks:
        g = at(g_s, i, jb)
        if jb == i // size:
            square = square + g * g
            trace = trace + jnp.where(sub == i % size, g, 0.0)
        else:
            cross = cross + g * g
    square = square + 2.0 * cross
    base = members - 1.0
    total = (
        base * base * members
        + 2.0 * base * jnp.sum(trace, axis=0, keepdims=True)
        + jnp.sum(square, axis=0, keepdims=True)
    )
    scale = jnp.sqrt(total)
    inv = 1.0 / scale
    a_coef = full(base * inv)

    z = 1.5 - 0.5 * a_coef
    for i, jb in blocks:
        g = at(g_s, i, jb) * inv
        put(g_s, i, jb, g)
        m, r = zero, -0.5 * g
        if jb == i // size:
            here = sub == i % size
            m = jnp.where(here, -0.5, 0.0)
            r = r + jnp.where(here, z, 0.0)
        upper(m_s, i, jb, m)
        put(r_s, i, jb, r)
        upper(q_s, i, jb, a_coef * m + r)

    for it in range(1, NS_ITERS):
        last = it == NS_ITERS - 1
        t = 1.5 - 0.5 * a_coef * z * z

        def tmat(i, jb, v):
            upper(t_s, i, jb, -0.5 * (v + z * (at(q_s, i, jb) - at(r_s, i, jb))))

        product(q_s, r_s, tmat)

        def mmat(i, jb, v):
            m = t * at(m_s, i, jb) + v
            if last:
                put(m_s, i, jb, m * inv)
            else:
                upper(m_s, i, jb, m)

        product(t_s, r_s, mmat)
        z = t * z
        if not last:

            def rmat(i, jb, v):
                if jb == i // size:
                    v = v + jnp.where(sub == i % size, z, 0.0)
                put(r_s, i, jb, v)
                upper(q_s, i, jb, a_coef * at(m_s, i, jb) + v)

            product(m_s, g_s, rmat)

    root = full(lax.rsqrt(scale))

    def cmat(step, carry):
        for g0 in range(0, groups, 4):
            acc = [zero] * 16
            for k in range(order):
                b = [bl_s[pl.ds(k * members + (g0 + g) * size, size), :] for g in range(4)]
                for i in range(4):
                    lhs = row_of(m_s, k * order + step * 4 + i)
                    for g in range(4):
                        acc[i * 4 + g] = acc[i * 4 + g] + lhs * b[g]
            for i in range(4):
                for g in range(4):
                    start = (step * 4 + i) * members + (g0 + g) * size
                    c_s[pl.ds(pl.multiple_of(start, size), size), :] = acc[i * 4 + g]
        return carry

    lax.fori_loop(0, order // 4, cmat, 0)

    def smat_times(vector):
        for g in range(groups):
            t_s[pl.ds(g * size, size), :] = vector[g]
        down = [zero] * nb
        for k in range(members):
            v = row_of(t_s, k)
            for j in range(nb):
                down[j] = down[j] + v * bk_s[pl.ds(k * order + j * size, size), :]
        for j in range(nb):
            t_s[pl.ds(members + j * size, size), :] = down[j]
        up = [z * vector[g] for g in range(groups)]
        for l in range(order):
            u = row_of(t_s, members + l)
            for g in range(groups):
                up[g] = up[g] + u * c_s[pl.ds(l * members + g * size, size), :]
        return [root * up[g] for g in range(groups)]

    wbar = smat_times(smat_times(vec))
    for g in range(groups):
        t_s[pl.ds(g * size, size), :] = wbar[g]

    gain = full(jnp.float32(base) ** 0.5 * root)

    half = members // 2

    def vmat(step, carry):
        ks = [2 * step, 2 * step + 1, half + 2 * step, half + 2 * step + 1]
        slabs = [[], [], [], []]
        for g0 in range(0, groups, 4):
            acc = [zero] * 16
            for l in range(order):
                c = [c_s[pl.ds(l * members + (g0 + g) * size, size), :] for g in range(4)]
                for i in range(4):
                    lhs = row_of(bk_s, ks[i] * order + l)
                    for g in range(4):
                        acc[i * 4 + g] = acc[i * 4 + g] + lhs * c[g]
            for i in range(4):
                for g in range(4):
                    here = sub + (g0 + g) * size == ks[i]
                    s = gain * (acc[i * 4 + g] + jnp.where(here, z, 0.0))
                    s = s + t_s[pl.ds((g0 + g) * size, size), :]
                    slabs[i].append(s - jnp.where(here, 1.0, 0.0))
        for i in range(2):
            both = jnp.concatenate(slabs[i] + slabs[2 + i], axis=0)
            start = pl.multiple_of(ks[i] * LANES, LANES)
            w_s[pl.ds(start, LANES), :] = jnp.transpose(both)
        return carry

    lax.fori_loop(0, half // 2, vmat, 0)
    load.wait()

    def apply(pair, carry):
        region, place = pair // (size // 2), pair % (size // 2)
        start = pl.multiple_of(place * 2 * size, 2 * size)
        outs = []
        for second, x in enumerate(point_rows(ens_ref, region, start)):
            x = (x - jnp.mean(x, axis=0, keepdims=True)).astype(BF16)
            gap = jnp.zeros_like(x)
            rhs = jnp.concatenate(
                [jnp.concatenate([x, gap], axis=1), jnp.concatenate([gap, x], axis=1)], axis=0
            )
            lhs = w_s[pl.ds(pair * 2 + second, half, stride=LANES), :].astype(BF16)
            outs.append(dot(lhs, rhs))
        for g in range(groups):
            top, side = g * size % half, g * size // half
            piece = [
                o[top : top + size, side * LANES : (side + 1) * LANES] for o in outs
            ]
            inc_ref[g, region, pl.ds(start, 2 * size), :] = jnp.concatenate(
                piece, axis=0
            ).astype(BF16)
        return carry

    steps = 4
    some = regions // steps
    stores = []
    for c in range(steps):
        lax.fori_loop(c * some * size // 2, (c + 1) * some * size // 2, apply, 0, unroll=8)
        span = pl.ds(c * some, some)
        stores.append(
            pltpu.make_async_copy(inc_ref.at[:, span], inc_hbm.at[:, span], out_sem.at[c])
        )
        stores[c].start()
    for copy in stores:
        copy.wait()


def analyse(before, own, after, nbr, loc, ens):
    order, points = nbr.shape
    members = ens.shape[0] * 8
    hbm = pl.BlockSpec(memory_space=pl.ANY)
    small = pltpu.VMEM((order * order, LANES), F32)
    tall = pltpu.VMEM((order * members, LANES), F32)
    return pl.pallas_call(
        analyse_kernel,
        out_shape=jax.ShapeDtypeStruct(ens.shape, BF16),
        in_specs=[VM] * 5 + [hbm],
        out_specs=hbm,
        scratch_shapes=[
            pltpu.VMEM(ens.shape, BF16),
            pltpu.VMEM(ens.shape, BF16),
            pltpu.VMEM((members + 16, 3 * own.shape[1]), BF16),
            tall,
            tall,
            small,
            small,
            small,
            small,
            small,
            tall,
            pltpu.VMEM((members // 2 * LANES, LANES), F32),
            pltpu.SemaphoreType.DMA((1,)),
            pltpu.SemaphoreType.DMA((4,)),
        ],
        compiler_params=pltpu.CompilerParams(vmem_limit_bytes=56 * 2**20),
        name="analyse",
    )(before, own, after, nbr, loc, ens)


def finish_kernel(fore_ref, inc_ref, out_ref, sum_s):
    members, grid_r, _ = out_ref.shape
    tiles, rows, _ = fore_ref.shape

    def add(t, carry):
        sum_s[pl.ds(pl.multiple_of(t * rows, rows), rows), :] = fore_ref[t].astype(F32) + inc_ref[
            t
        ].astype(F32)
        return carry

    lax.fori_loop(0, tiles, add, 0, unroll=4)
    for k in range(members):
        out_ref[k] = sum_s[pl.ds(k, grid_r, stride=members), :].astype(BF16)


def finish(fore, inc, members):
    tiles, rows, _ = fore.shape
    grid_r = tiles * rows // members
    return pl.pallas_call(
        finish_kernel,
        out_shape=jax.ShapeDtypeStruct((members, grid_r, LANES), BF16),
        in_specs=[VM, VM],
        out_specs=VM,
        scratch_shapes=[pltpu.VMEM((tiles * rows, LANES), F32)],
        compiler_params=pltpu.CompilerParams(vmem_limit_bytes=40 * 2**20),
        name="finish",
    )(fore, inc)


def neighbours(inner, outer, axis, wrap):
    count = lax.axis_size(axis)
    within = [(i, i ^ 1) for i in range(count)]
    links = [(i, (i + 1) % count) for i in range(1, count if wrap else count - 1, 2)]
    across = links + [(b, a) for a, b in links]
    got = lax.ppermute(outer, axis, across)
    return lax.ppermute(inner, axis, within), got


def swapped(index, low, high, odd):
    moved = jnp.where(index < low, index + high, jnp.where(index >= high, index - high, index))
    return jnp.where(odd == 1, moved, index)


def exchange(blocks):
    return lax.all_to_all(blocks, MR, split_axis=0, concat_axis=0, tiled=True)


def shards(
    latent_vertex_values,
    background_field,
    edge_senders,
    grid_parent,
    w_send,
    w_recv,
    w_node,
    w_agg,
    w_out,
    norm_gain,
    w_dec,
    obs_loc,
    obs_count,
    obs_value,
    obs_var,
    obs_nbr,
    loc_weight,
):
    members, nodes, width = latent_vertex_values.shape
    grid_r = background_field.shape[1]
    groups, regions = lax.axis_size("member"), lax.axis_size("region")

    def node_major(array):
        return array.transpose(1, 0, 2).reshape(-1, array.shape[2])

    odd = lax.axis_index("region") % 2

    def rim(start):
        return node_major(lax.dynamic_slice_in_dim(latent_vertex_values, start, RIM, 1))

    inner, outer = neighbours(
        rim(jnp.where(odd == 1, 0, nodes - RIM)),
        rim(jnp.where(odd == 1, nodes - RIM, 0)),
        "region",
        True,
    )
    edges = swapped(edge_senders - (nodes - RIM), RIM, nodes + RIM, odd)
    weights = (w_send, w_recv, w_node, w_agg, w_out, norm_gain[None], w_dec)
    processed, fore = forecast(
        node_major(latent_vertex_values),
        outer,
        inner,
        node_major(background_field),
        edges,
        grid_parent,
        weights,
    )
    processed = processed.reshape(nodes, members, width).transpose(1, 0, 2)
    ens = exchange(fore)
    ens = ens.reshape(groups, regions, *ens.shape[1:])
    payload = observe(ens, obs_loc, obs_count, obs_value, obs_var)
    pay_inner, pay_outer = neighbours(payload, payload, MR, False)
    slots = obs_loc.shape[0]
    nbr = swapped(obs_nbr, slots, 2 * slots, odd)
    inc = analyse(pay_outer, payload, pay_inner, nbr, loc_weight, ens)
    landed = exchange(inc.reshape(groups * regions, *inc.shape[2:]))
    return processed, finish(fore, landed, members)


def solution(mesh):
    in_specs = (
        P("member", "region", None),
        P("member", "region", None),
        P("region", None),
        P("region"),
        P(),
        P(),
        P(),
        P(),
        P(),
        P(),
        P(),
        P(MR),
        P(MR),
        P(MR),
        P(MR),
        P(None, MR),
        P(None, MR),
    )
    out_specs = (P("member", "region", None), P("member", "region", None))
    return jax.shard_map(shards, mesh=mesh, in_specs=in_specs, out_specs=out_specs, check_vma=False)
```

```python
import functools

import jax
import jax.numpy as jnp
from jax import lax
from jax.experimental import pallas as pl
from jax.experimental.pallas import tpu as pltpu
from jax.sharding import PartitionSpec as P

NS_ITERS = 6
LANES = 128
RIM = 64
MEMBERS = 8
GROUP = 8
CHUNKS = 4
UNROLL = 8
F32 = jnp.float32
BF16 = jnp.bfloat16
MR = ("member", "region")
VM = pl.BlockSpec(memory_space=pltpu.VMEM)
SM = pl.BlockSpec(memory_space=pltpu.SMEM)


def dot(a, b):
    return jnp.dot(a, b, preferred_element_type=F32)


def forecast_kernel(
    edge_ref,
    parent_ref,
    latent_hbm,
    before_ref,
    after_ref,
    back_hbm,
    w_send_ref,
    w_recv_ref,
    w_node_hbm,
    w_agg_hbm,
    w_out_hbm,
    gain_ref,
    w_dec_hbm,
    proc_hbm,
    fore_hbm,
    send_s,
    recv_s,
    dec_s,
    raw_s,
    latent_s,
    back_s,
    proc_s,
    fore_s,
    w_node_s,
    w_agg_s,
    w_out_s,
    w_dec_s,
    in_sem,
    out_sem,
):
    members, nodes, width = latent_hbm.shape
    count = members * nodes
    rim = before_ref.shape[0]
    degree = edge_ref.shape[0] // nodes
    rows = count // CHUNKS
    tile = members * GROUP

    def piece(c):
        return pl.ds(c * rows, rows)

    def own(c):
        return pl.ds(c * (nodes // CHUNKS), nodes // CHUNKS)

    def node_rows(array):
        return jnp.swapaxes(array.astype(F32), 0, 1).reshape(-1, array.shape[2]).astype(BF16)

    loads = [
        pltpu.make_async_copy(latent_hbm.at[:, own(c)], raw_s.at[:, own(c)], in_sem.at[c])
        for c in range(CHUNKS)
    ]
    later = [
        pltpu.make_async_copy(src, dst, in_sem.at[CHUNKS + i])
        for i, (src, dst) in enumerate(
            [
                (w_node_hbm, w_node_s),
                (w_agg_hbm, w_agg_s),
                (w_out_hbm, w_out_s),
                (w_dec_hbm, w_dec_s),
                (back_hbm, back_s),
            ]
        )
    ]
    for copy in loads + later:
        copy.start()

    def send_of(state):
        return dot(state, w_send_ref[...]).astype(BF16).astype(F32) * 0.5

    cols = width // LANES

    def spread_rows(ref, first, values):
        for c in range(cols):
            part = values[:, c * LANES : (c + 1) * LANES].reshape(-1, members, LANES)
            ref[first // members : first // members + part.shape[0], c] = part

    spread_rows(send_s, 0, send_of(before_ref[...]))
    spread_rows(send_s, rim + count, send_of(after_ref[...]))
    for c in range(CHUNKS):
        loads[c].wait()
        state = node_rows(raw_s[:, own(c)])
        latent_s[piece(c)] = state
        spread_rows(send_s, rim + c * rows, send_of(state))
        spread_rows(recv_s, c * rows, dot(state, w_recv_ref[...]) * 0.5)

    def aggregate(n, carry):
        mine = recv_s[n]
        total = jnp.zeros_like(mine)
        for e in range(degree):
            half = send_s[edge_ref[n * degree + e]] + mine
            total = total + (half + half * jnp.tanh(half))
        recv_s[n] = total
        return carry

    lax.fori_loop(0, nodes, aggregate, 0, unroll=8)
    for copy in later:
        copy.wait()

    def store_proc(c):
        return pltpu.make_async_copy(proc_s.at[piece(c)], proc_hbm.at[piece(c)], out_sem.at[c])

    def update(c):
        state = latent_s[piece(c)]
        some_nodes = pl.ds(c * (rows // members), rows // members)
        agg = jnp.concatenate(
            [recv_s[some_nodes, i].reshape(rows, LANES) for i in range(cols)], axis=1
        ).astype(BF16)
        pre = (dot(state, w_node_s[...]) + dot(agg, w_agg_s[...])) * 0.5
        hidden = (pre + pre * jnp.tanh(pre)).astype(BF16)
        out = dot(hidden, w_out_s[...])
        mean = jnp.mean(out, axis=-1, keepdims=True)
        centred = out - mean
        var = jnp.mean(centred * centred, axis=-1, keepdims=True)
        norm = centred * lax.rsqrt(var + 1e-05) * gain_ref[...]
        proc = (state.astype(F32) + norm).astype(BF16)
        proc_s[piece(c)] = proc
        store_proc(c).start()
        dec_s[some_nodes] = dot(proc, w_dec_s[...]).reshape(-1, members, LANES)

    for c in range(CHUNKS):
        update(c)

    tiles = fore_s.shape[0]
    some = tiles // CHUNKS

    def store_fore(c):
        span = pl.ds(c * some, some)
        return pltpu.make_async_copy(fore_s.at[span], fore_hbm.at[span], out_sem.at[CHUNKS + c])

    for c in range(CHUNKS):

        def spread(pair, carry):
            back = back_s[:, pl.ds(pl.multiple_of(pair * 2 * GROUP, 2 * GROUP), 2 * GROUP), :]
            back = jnp.swapaxes(back.astype(F32), 0, 1).reshape(2 * tile, LANES)
            for i in range(2):
                t = pair * 2 + i
                parts = [dec_s[parent_ref[t * GROUP + q]] for q in range(GROUP)]
                values = jnp.concatenate(parts, axis=0) + back[i * tile : (i + 1) * tile]
                fore_s[t] = values.astype(BF16)
            return carry

        lax.fori_loop(c * some // 2, (c + 1) * some // 2, spread, 0, unroll=4)
        store_fore(c).start()

    for c in range(CHUNKS):
        store_proc(c).wait()
        store_fore(c).wait()


def forecast(latent, before, after, back, senders, parent, weights):
    members, nodes, width = latent.shape
    count = members * nodes
    grid_rows = members * back.shape[1]
    rim = before.shape[0]
    tiles = lax.axis_size("member") * lax.axis_size("region")
    hbm = pl.BlockSpec(memory_space=pl.ANY)
    w_shape = pltpu.VMEM(weights[2].shape, BF16)
    return pl.pallas_call(
        forecast_kernel,
        out_shape=(
            jax.ShapeDtypeStruct((count, width), BF16),
            jax.ShapeDtypeStruct((tiles, grid_rows // tiles, LANES), BF16),
        ),
        in_specs=[SM, SM, hbm, VM, VM, hbm, VM, VM, hbm, hbm, hbm, VM, hbm],
        out_specs=(hbm, hbm),
        scratch_shapes=[
            pltpu.VMEM(((count + 2 * rim) // MEMBERS, width // LANES, MEMBERS, LANES), F32),
            pltpu.VMEM((count // MEMBERS, width // LANES, MEMBERS, LANES), F32),
            pltpu.VMEM((count // MEMBERS, MEMBERS, LANES), F32),
            pltpu.VMEM(latent.shape, BF16),
            pltpu.VMEM((count, width), BF16),
            pltpu.VMEM(back.shape, BF16),
            pltpu.VMEM((count, width), BF16),
            pltpu.VMEM((tiles, grid_rows // tiles, LANES), BF16),
            w_shape,
            w_shape,
            w_shape,
            pltpu.VMEM(weights[6].shape, BF16),
            pltpu.SemaphoreType.DMA((CHUNKS + 5,)),
            pltpu.SemaphoreType.DMA((2 * CHUNKS,)),
        ],
        compiler_params=pltpu.CompilerParams(vmem_limit_bytes=56 * 2**20),
        name="forecast",
    )(senders.reshape(-1), parent, latent, before, after, back, *weights)


def point_rows(ens_ref, region, start):
    size = 8
    blocks = [
        ens_ref[g, region, pl.ds(start, 2 * size), :].astype(F32) for g in range(ens_ref.shape[0])
    ]
    return [
        jnp.concatenate([b[i * size : (i + 1) * size] for b in blocks], axis=0) for i in range(2)
    ]


def observe_kernel(count_ref, loc_ref, ens_ref, value_ref, var_ref, pay_ref):
    groups, regions, rows, _ = ens_ref.shape
    size = 8
    members = groups * size
    slots = loc_ref.shape[1]
    pairs = size // 2
    loc = loc_ref[...]
    flat = loc % LANES * LANES + loc // LANES
    entry = lax.broadcasted_iota(jnp.int32, (2 * LANES, slots), 0)

    def add(pair, acc):
        start = pl.multiple_of(pair % pairs * 2 * size, 2 * size)
        state = jnp.concatenate(point_rows(ens_ref, pair // pairs, start), axis=1).astype(BF16)
        chosen = jnp.where(entry == flat - pair * 2 * LANES, 1.0, 0.0).astype(BF16)
        return acc + dot(state, chosen)

    yens = lax.fori_loop(0, regions * pairs, add, jnp.zeros((members, slots), F32), unroll=8)
    ybar = jnp.mean(yens, axis=0, keepdims=True)
    slot = lax.broadcasted_iota(jnp.int32, (1, slots), 1)
    rinv = jnp.where(slot < count_ref[0], 1.0, 0.0) / var_ref[...]
    dres = (value_ref[...] - ybar) * rinv
    row = lax.broadcasted_iota(jnp.int32, (16, slots), 0)
    extra = jnp.where(row == 0, rinv, jnp.where(row == 1, dres, 0.0))
    pay_ref[0:members] = (yens - ybar).astype(BF16)
    pay_ref[members : members + 16] = extra.astype(BF16)


def observe(ens, loc, count, value, var):
    groups, regions, rows, _ = ens.shape
    return pl.pallas_call(
        observe_kernel,
        out_shape=jax.ShapeDtypeStruct((groups * 8 + 16, loc.shape[0]), BF16),
        in_specs=[SM, VM, VM, VM, VM],
        out_specs=VM,
        compiler_params=pltpu.CompilerParams(vmem_limit_bytes=40 * 2**20),
        name="observe",
    )(count, loc[None], ens, value[None], var[None])


def analyse_kernel(
    before_ref,
    own_ref,
    after_ref,
    nbr_ref,
    loc_ref,
    ens_hbm,
    inc_hbm,
    ens_ref,
    inc_ref,
    pay_s,
    bl_s,
    bk_s,
    g_s,
    m_s,
    r_s,
    q_s,
    t_s,
    c_s,
    w_s,
    in_sem,
    out_sem,
):
    groups, regions, rows, _ = ens_ref.shape
    load = pltpu.make_async_copy(ens_hbm, ens_ref, in_sem.at[0])
    load.start()
    size = 8
    members = groups * size
    order = nbr_ref.shape[0]
    nb = order // size
    slots = own_ref.shape[1]
    sub = lax.broadcasted_iota(jnp.int32, (size, LANES), 0)

    for i, ref in enumerate((before_ref, own_ref, after_ref)):
        pay_s[:, i * slots : (i + 1) * slots] = ref[...]

    def full(row):
        return jnp.broadcast_to(row, (size, LANES))

    entry = lax.broadcasted_iota(jnp.int32, (3 * slots, 2 * LANES), 0)

    def gather(step, vec):
        index = jnp.concatenate(
            [nbr_ref[pl.ds(2 * step, 1), :], nbr_ref[pl.ds(2 * step + 1, 1), :]], axis=1
        )
        chosen = jnp.where(entry == index, 1.0, 0.0).astype(BF16)
        both = dot(pay_s[...], chosen)
        vec = list(vec)
        for i in range(2):
            l = 2 * step + i
            panel = both[:, i * LANES : (i + 1) * LANES]
            weight = loc_ref[pl.ds(l, 1), :]
            root = jnp.sqrt(weight * panel[members : members + 1])
            dl = weight * panel[members + 1 : members + 2]
            for g in range(groups):
                yl = panel[g * size : (g + 1) * size]
                vec[g] = vec[g] + yl * dl
                b = yl * root
                bl_s[pl.ds(pl.multiple_of(l * members + g * size, size), size), :] = b
                bk_s[pl.ds(g * size * order + l, size, stride=order), :] = b
        return tuple(vec)

    zero = jnp.zeros((size, LANES), F32)
    vec = lax.fori_loop(0, order // 2, gather, tuple([zero] * groups), unroll=2)

    def row_of(ref, r):
        return jnp.broadcast_to(ref[pl.ds(r, 1), :], (size, LANES))

    def accumulate(start, stop, left_row, right, a, acc):
        width = nb - a

        def body(k, acc):
            rhs = [
                right[pl.ds(pl.multiple_of(k * order + (a + j) * size, size), size), :]
                for j in range(width)
            ]
            out = []
            for i in range(size):
                lhs = left_row(k, i)
                for j in range(width):
                    out.append(acc[i * width + j] + lhs * rhs[j])
            return tuple(out)

        return lax.fori_loop(start, stop, body, acc, unroll=UNROLL)

    def finish_group(a, acc, finish):
        width = nb - a
        for i in range(size):
            for j in range(width):
                finish(a * size + i, a + j, acc[i * width + j])

    def gram(ref, count, finish):
        for a in range(nb):
            acc = accumulate(
                0,
                count,
                lambda k, i: row_of(ref, k * order + a * size + i),
                ref,
                a,
                tuple([zero] * (size * (nb - a))),
            )
            finish_group(a, acc, finish)

    def product(left, right, finish):
        for a in range(nb):
            edge = (a + 1) * size
            acc = accumulate(
                0,
                edge,
                lambda k, i: row_of(left, k * order + a * size + i),
                right,
                a,
                tuple([zero] * (size * (nb - a))),
            )
            if edge < order:
                acc = accumulate(
                    edge,
                    order,
                    lambda k, i: row_of(left, (a * size + i) * order + k),
                    right,
                    a,
                    acc,
                )
            finish_group(a, acc, finish)

    def at(ref, i, jb):
        return ref[pl.ds(i * order + jb * size, size), :]

    def put(ref, i, jb, value):
        ref[pl.ds(i * order + jb * size, size), :] = value
        if jb != i // size:
            ref[pl.ds(jb * size * order + i, size, stride=order), :] = value

    def upper(ref, i, jb, value):
        ref[pl.ds(i * order + jb * size, size), :] = value

    blocks = [(i, jb) for i in range(order) for jb in range(i // size, nb)]
    gram(bk_s, members, functools.partial(upper, g_s))

    square, cross, trace = zero, zero, zero
    for i, jb in blocks:
        g = at(g_s, i, jb)
        if jb == i // size:
            square = square + g * g
            trace = trace + jnp.where(sub == i % size, g, 0.0)
        else:
            cross = cross + g * g
    square = square + 2.0 * cross
    base = members - 1.0
    total = (
        base * base * members
        + 2.0 * base * jnp.sum(trace, axis=0, keepdims=True)
        + jnp.sum(square, axis=0, keepdims=True)
    )
    scale = jnp.sqrt(total)
    inv = 1.0 / scale
    a_coef = full(base * inv)

    z = 1.5 - 0.5 * a_coef
    for i, jb in blocks:
        g = at(g_s, i, jb) * inv
        put(g_s, i, jb, g)
        m, r = zero, -0.5 * g
        if jb == i // size:
            here = sub == i % size
            m = jnp.where(here, -0.5, 0.0)
            r = r + jnp.where(here, z, 0.0)
        upper(m_s, i, jb, m)
        put(r_s, i, jb, r)
        upper(q_s, i, jb, a_coef * m + r)

    for it in range(1, NS_ITERS):
        last = it == NS_ITERS - 1
        t = 1.5 - 0.5 * a_coef * z * z

        def tmat(i, jb, v):
            upper(t_s, i, jb, -0.5 * (v + z * (at(q_s, i, jb) - at(r_s, i, jb))))

        product(q_s, r_s, tmat)

        def mmat(i, jb, v):
            m = t * at(m_s, i, jb) + v
            if last:
                put(m_s, i, jb, m * inv)
            else:
                upper(m_s, i, jb, m)

        product(t_s, r_s, mmat)
        z = t * z
        if not last:

            def rmat(i, jb, v):
                if jb == i // size:
                    v = v + jnp.where(sub == i % size, z, 0.0)
                put(r_s, i, jb, v)
                upper(q_s, i, jb, a_coef * at(m_s, i, jb) + v)

            product(m_s, g_s, rmat)

    root = full(lax.rsqrt(scale))

    def cmat(step, carry):
        for g0 in range(0, groups, 4):
            acc = [zero] * 16
            for k in range(order):
                b = [bl_s[pl.ds(k * members + (g0 + g) * size, size), :] for g in range(4)]
                for i in range(4):
                    lhs = row_of(m_s, k * order + step * 4 + i)
                    for g in range(4):
                        acc[i * 4 + g] = acc[i * 4 + g] + lhs * b[g]
            for i in range(4):
                for g in range(4):
                    start = (step * 4 + i) * members + (g0 + g) * size
                    c_s[pl.ds(pl.multiple_of(start, size), size), :] = acc[i * 4 + g]
        return carry

    lax.fori_loop(0, order // 4, cmat, 0)

    def smat_times(vector):
        for g in range(groups):
            t_s[pl.ds(g * size, size), :] = vector[g]
        down = [zero] * nb
        for k in range(members):
            v = row_of(t_s, k)
            for j in range(nb):
                down[j] = down[j] + v * bk_s[pl.ds(k * order + j * size, size), :]
        for j in range(nb):
            t_s[pl.ds(members + j * size, size), :] = down[j]
        up = [z * vector[g] for g in range(groups)]
        for l in range(order):
            u = row_of(t_s, members + l)
            for g in range(groups):
                up[g] = up[g] + u * c_s[pl.ds(l * members + g * size, size), :]
        return [root * up[g] for g in range(groups)]

    wbar = smat_times(smat_times(vec))
    for g in range(groups):
        t_s[pl.ds(g * size, size), :] = wbar[g]

    gain = full(jnp.float32(base) ** 0.5 * root)

    half = members // 2

    def vmat(step, carry):
        ks = [2 * step, 2 * step + 1, half + 2 * step, half + 2 * step + 1]
        slabs = [[], [], [], []]
        for g0 in range(0, groups, 4):
            acc = [zero] * 16
            for l in range(order):
                c = [c_s[pl.ds(l * members + (g0 + g) * size, size), :] for g in range(4)]
                for i in range(4):
                    lhs = row_of(bk_s, ks[i] * order + l)
                    for g in range(4):
                        acc[i * 4 + g] = acc[i * 4 + g] + lhs * c[g]
            for i in range(4):
                for g in range(4):
                    here = sub + (g0 + g) * size == ks[i]
                    s = gain * (acc[i * 4 + g] + jnp.where(here, z, 0.0))
                    s = s + t_s[pl.ds((g0 + g) * size, size), :]
                    slabs[i].append(s - jnp.where(here, 1.0, 0.0))
        for i in range(2):
            both = jnp.concatenate(slabs[i] + slabs[2 + i], axis=0)
            start = pl.multiple_of(ks[i] * LANES, LANES)
            w_s[pl.ds(start, LANES), :] = jnp.transpose(both)
        return carry

    lax.fori_loop(0, half // 2, vmat, 0)
    load.wait()

    def apply(pair, carry):
        region, place = pair // (size // 2), pair % (size // 2)
        start = pl.multiple_of(place * 2 * size, 2 * size)
        outs = []
        for second, x in enumerate(point_rows(ens_ref, region, start)):
            x = (x - jnp.mean(x, axis=0, keepdims=True)).astype(BF16)
            gap = jnp.zeros_like(x)
            rhs = jnp.concatenate(
                [jnp.concatenate([x, gap], axis=1), jnp.concatenate([gap, x], axis=1)], axis=0
            )
            lhs = w_s[pl.ds(pair * 2 + second, half, stride=LANES), :].astype(BF16)
            outs.append(dot(lhs, rhs))
        for g in range(groups):
            top, side = g * size % half, g * size // half
            piece = [
                o[top : top + size, side * LANES : (side + 1) * LANES] for o in outs
            ]
            inc_ref[g, region, pl.ds(start, 2 * size), :] = jnp.concatenate(
                piece, axis=0
            ).astype(BF16)
        return carry

    steps = 4
    some = regions // steps
    stores = []
    for c in range(steps):
        lax.fori_loop(c * some * size // 2, (c + 1) * some * size // 2, apply, 0, unroll=8)
        span = pl.ds(c * some, some)
        stores.append(
            pltpu.make_async_copy(inc_ref.at[:, span], inc_hbm.at[:, span], out_sem.at[c])
        )
        stores[c].start()
    for copy in stores:
        copy.wait()


def analyse(before, own, after, nbr, loc, ens):
    order, points = nbr.shape
    members = ens.shape[0] * 8
    hbm = pl.BlockSpec(memory_space=pl.ANY)
    small = pltpu.VMEM((order * order, LANES), F32)
    tall = pltpu.VMEM((order * members, LANES), F32)
    return pl.pallas_call(
        analyse_kernel,
        out_shape=jax.ShapeDtypeStruct(ens.shape, BF16),
        in_specs=[VM] * 5 + [hbm],
        out_specs=hbm,
        scratch_shapes=[
            pltpu.VMEM(ens.shape, BF16),
            pltpu.VMEM(ens.shape, BF16),
            pltpu.VMEM((members + 16, 3 * own.shape[1]), BF16),
            tall,
            tall,
            small,
            small,
            small,
            small,
            small,
            tall,
            pltpu.VMEM((members // 2 * LANES, LANES), F32),
            pltpu.SemaphoreType.DMA((1,)),
            pltpu.SemaphoreType.DMA((4,)),
        ],
        compiler_params=pltpu.CompilerParams(vmem_limit_bytes=56 * 2**20),
        name="analyse",
    )(before, own, after, nbr, loc, ens)


def finish_kernel(fore_hbm, inc_hbm, out_hbm, fore_s, inc_s, out_s, in_sem, out_sem):
    members, grid_r, _ = out_s.shape
    tiles, rows, _ = fore_s.shape
    steps = in_sem.shape[0] // 2
    some, points = tiles // steps, grid_r // steps

    def loads(c):
        span = pl.ds(c * some, some)
        return [
            pltpu.make_async_copy(fore_hbm.at[span], fore_s.at[span], in_sem.at[c]),
            pltpu.make_async_copy(inc_hbm.at[span], inc_s.at[span], in_sem.at[steps + c]),
        ]

    def store(c):
        span = pl.ds(c * points, points)
        return pltpu.make_async_copy(out_s.at[:, span], out_hbm.at[:, span], out_sem.at[c])

    for c in range(steps):
        for copy in loads(c):
            copy.start()
    for c in range(steps):
        for copy in loads(c):
            copy.wait()
        span = pl.ds(c * some, some)
        total = fore_s[span].astype(F32) + inc_s[span].astype(F32)
        total = jnp.swapaxes(total.reshape(points, members, LANES), 0, 1)
        out_s[:, pl.ds(c * points, points), :] = total.astype(BF16)
        store(c).start()
    for c in range(steps):
        store(c).wait()


def finish(fore, inc, members):
    tiles, rows, _ = fore.shape
    shape = (members, tiles * rows // members, LANES)
    steps = 8
    hbm = pl.BlockSpec(memory_space=pl.ANY)
    return pl.pallas_call(
        finish_kernel,
        out_shape=jax.ShapeDtypeStruct(shape, BF16),
        in_specs=[hbm, hbm],
        out_specs=hbm,
        scratch_shapes=[
            pltpu.VMEM(fore.shape, BF16),
            pltpu.VMEM(fore.shape, BF16),
            pltpu.VMEM(shape, BF16),
            pltpu.SemaphoreType.DMA((2 * steps,)),
            pltpu.SemaphoreType.DMA((steps,)),
        ],
        compiler_params=pltpu.CompilerParams(vmem_limit_bytes=40 * 2**20),
        name="finish",
    )(fore, inc)


def neighbours(inner, outer, axis, wrap):
    count = lax.axis_size(axis)
    within = [(i, i ^ 1) for i in range(count)]
    links = [(i, (i + 1) % count) for i in range(1, count if wrap else count - 1, 2)]
    across = links + [(b, a) for a, b in links]
    got = lax.ppermute(outer, axis, across)
    return lax.ppermute(inner, axis, within), got


def swapped(index, low, high, odd):
    moved = jnp.where(index < low, index + high, jnp.where(index >= high, index - high, index))
    return jnp.where(odd == 1, moved, index)


def exchange(blocks):
    return lax.all_to_all(blocks, MR, split_axis=0, concat_axis=0, tiled=True)


def shards(
    latent_vertex_values,
    background_field,
    edge_senders,
    grid_parent,
    w_send,
    w_recv,
    w_node,
    w_agg,
    w_out,
    norm_gain,
    w_dec,
    obs_loc,
    obs_count,
    obs_value,
    obs_var,
    obs_nbr,
    loc_weight,
):
    members, nodes, width = latent_vertex_values.shape
    grid_r = background_field.shape[1]
    groups, regions = lax.axis_size("member"), lax.axis_size("region")

    def node_major(array):
        return array.transpose(1, 0, 2).reshape(-1, array.shape[2])

    odd = lax.axis_index("region") % 2

    def rim(start):
        return node_major(lax.dynamic_slice_in_dim(latent_vertex_values, start, RIM, 1))

    inner, outer = neighbours(
        rim(jnp.where(odd == 1, 0, nodes - RIM)),
        rim(jnp.where(odd == 1, nodes - RIM, 0)),
        "region",
        True,
    )
    edges = swapped(edge_senders - (nodes - RIM), RIM, nodes + RIM, odd)
    weights = (w_send, w_recv, w_node, w_agg, w_out, norm_gain[None], w_dec)
    processed, fore = forecast(
        latent_vertex_values,
        outer,
        inner,
        background_field,
        edges,
        grid_parent,
        weights,
    )
    processed = processed.reshape(nodes, members, width).transpose(1, 0, 2)
    ens = exchange(fore)
    ens = ens.reshape(groups, regions, *ens.shape[1:])
    payload = observe(ens, obs_loc, obs_count, obs_value, obs_var)
    pay_inner, pay_outer = neighbours(payload, payload, MR, False)
    slots = obs_loc.shape[0]
    nbr = swapped(obs_nbr, slots, 2 * slots, odd)
    inc = analyse(pay_outer, payload, pay_inner, nbr, loc_weight, ens)
    landed = exchange(inc.reshape(groups * regions, *inc.shape[2:]))
    return processed, finish(fore, landed, members)


def solution(mesh):
    in_specs = (
        P("member", "region", None),
        P("member", "region", None),
        P("region", None),
        P("region"),
        P(),
        P(),
        P(),
        P(),
        P(),
        P(),
        P(),
        P(MR),
        P(MR),
        P(MR),
        P(MR),
        P(None, MR),
        P(None, MR),
    )
    out_specs = (P("member", "region", None), P("member", "region", None))
    return jax.shard_map(shards, mesh=mesh, in_specs=in_specs, out_specs=out_specs, check_vma=False)
```

```python
import functools

import jax
import jax.numpy as jnp
from jax import lax
from jax.experimental import pallas as pl
from jax.experimental.pallas import tpu as pltpu
from jax.sharding import PartitionSpec as P

NS_ITERS = 6
LANES = 128
RIM = 64
MEMBERS = 8
GROUP = 8
CHUNKS = 4
UNROLL = 8
F32 = jnp.float32
BF16 = jnp.bfloat16
MR = ("member", "region")
VM = pl.BlockSpec(memory_space=pltpu.VMEM)
SM = pl.BlockSpec(memory_space=pltpu.SMEM)


def dot(a, b):
    return jnp.dot(a, b, preferred_element_type=F32)


def lane_blocks(ref, first, values):
    for c in range(values.shape[1] // LANES):
        part = values[:, c * LANES : (c + 1) * LANES].reshape(-1, MEMBERS, LANES)
        ref[first // MEMBERS : first // MEMBERS + part.shape[0], c] = part


def project_kernel(
    latent_hbm,
    w_send_ref,
    w_recv_ref,
    state_hbm,
    send_hbm,
    recv_hbm,
    raw_s,
    state_s,
    send_s,
    recv_s,
    in_sem,
    out_sem,
):
    members, nodes, width = latent_hbm.shape
    some = nodes // CHUNKS
    rows = members * some

    def own(c):
        return pl.ds(c * some, some)

    def piece(c):
        return pl.ds(c * rows, rows)

    loads = [
        pltpu.make_async_copy(latent_hbm.at[:, own(c)], raw_s.at[:, own(c)], in_sem.at[c])
        for c in range(CHUNKS)
    ]
    for copy in loads:
        copy.start()
    stores = []
    for c in range(CHUNKS):
        loads[c].wait()
        turned = jnp.swapaxes(raw_s[:, own(c)].astype(F32), 0, 1)
        state = turned.reshape(rows, width).astype(BF16)
        state_s[piece(c)] = state
        send_s[piece(c)] = dot(state, w_send_ref[...]).astype(BF16)
        lane_blocks(recv_s, c * rows, dot(state, w_recv_ref[...]) * 0.5)
        pairs = [
            (state_s.at[piece(c)], state_hbm.at[piece(c)]),
            (send_s.at[piece(c)], send_hbm.at[piece(c)]),
            (recv_s.at[own(c)], recv_hbm.at[own(c)]),
        ]
        for k, (src, dst) in enumerate(pairs):
            copy = pltpu.make_async_copy(src, dst, out_sem.at[3 * c + k])
            copy.start()
            stores.append(copy)
    for copy in stores:
        copy.wait()


def project(latent, w_send, w_recv):
    members, nodes, width = latent.shape
    count = members * nodes
    flat = (count, width)
    blocks = (nodes, width // LANES, members, LANES)
    hbm = pl.BlockSpec(memory_space=pl.ANY)
    return pl.pallas_call(
        project_kernel,
        out_shape=(
            jax.ShapeDtypeStruct(flat, BF16),
            jax.ShapeDtypeStruct(flat, BF16),
            jax.ShapeDtypeStruct(blocks, F32),
        ),
        in_specs=[hbm, VM, VM],
        out_specs=(hbm, hbm, hbm),
        scratch_shapes=[
            pltpu.VMEM(latent.shape, BF16),
            pltpu.VMEM(flat, BF16),
            pltpu.VMEM(flat, BF16),
            pltpu.VMEM(blocks, F32),
            pltpu.SemaphoreType.DMA((CHUNKS,)),
            pltpu.SemaphoreType.DMA((3 * CHUNKS,)),
        ],
        compiler_params=pltpu.CompilerParams(vmem_limit_bytes=48 * 2**20),
        cost_estimate=pl.CostEstimate(
            flops=4 * count * width * width, bytes_accessed=10 * count * width, transcendentals=0
        ),
        name="project",
    )(latent, w_send, w_recv)


def forecast_kernel(
    edge_ref,
    parent_ref,
    latent_hbm,
    sent_hbm,
    recv_hbm,
    before_ref,
    after_ref,
    back_hbm,
    w_send_ref,
    w_node_hbm,
    w_agg_hbm,
    w_out_hbm,
    gain_ref,
    w_dec_hbm,
    proc_hbm,
    fore_hbm,
    send_s,
    recv_s,
    dec_s,
    sent_s,
    latent_s,
    back_s,
    proc_s,
    fore_s,
    w_node_s,
    w_agg_s,
    w_out_s,
    w_dec_s,
    in_sem,
    out_sem,
):
    nodes, cols, members, _ = recv_hbm.shape
    count, width = latent_hbm.shape
    rim = before_ref.shape[0]
    degree = edge_ref.shape[0] // nodes
    rows = count // CHUNKS
    tile = members * GROUP

    def piece(c):
        return pl.ds(c * rows, rows)

    def own(c):
        return pl.ds(c * (nodes // CHUNKS), nodes // CHUNKS)

    sent = [
        pltpu.make_async_copy(sent_hbm.at[piece(c)], sent_s.at[piece(c)], in_sem.at[c])
        for c in range(CHUNKS)
    ]
    mine = [
        pltpu.make_async_copy(recv_hbm.at[own(c)], recv_s.at[own(c)], in_sem.at[CHUNKS + c])
        for c in range(CHUNKS)
    ]
    later = [
        pltpu.make_async_copy(src, dst, in_sem.at[2 * CHUNKS + i])
        for i, (src, dst) in enumerate(
            [
                (latent_hbm, latent_s),
                (w_node_hbm, w_node_s),
                (w_agg_hbm, w_agg_s),
                (w_out_hbm, w_out_s),
                (w_dec_hbm, w_dec_s),
                (back_hbm, back_s),
            ]
        )
    ]
    for copy in sent + mine + later:
        copy.start()

    def rim_of(state):
        return dot(state, w_send_ref[...]).astype(BF16).astype(F32) * 0.5

    lane_blocks(send_s, 0, rim_of(before_ref[...]))
    lane_blocks(send_s, rim + count, rim_of(after_ref[...]))
    for c in range(CHUNKS):
        sent[c].wait()
        lane_blocks(send_s, rim + c * rows, sent_s[piece(c)].astype(F32) * 0.5)

    def aggregate(n, carry):
        mine = recv_s[n]
        total = jnp.zeros_like(mine)
        for e in range(degree):
            half = send_s[edge_ref[n * degree + e]] + mine
            total = total + (half + half * jnp.tanh(half))
        recv_s[n] = total
        return carry

    for c in range(CHUNKS):
        mine[c].wait()
        lax.fori_loop(c * nodes // CHUNKS, (c + 1) * nodes // CHUNKS, aggregate, 0, unroll=8)
    for copy in later:
        copy.wait()

    def store_proc(c):
        return pltpu.make_async_copy(proc_s.at[piece(c)], proc_hbm.at[piece(c)], out_sem.at[c])

    def update(c):
        state = latent_s[piece(c)]
        some_nodes = pl.ds(c * (rows // members), rows // members)
        agg = jnp.concatenate(
            [recv_s[some_nodes, i].reshape(rows, LANES) for i in range(cols)], axis=1
        ).astype(BF16)
        pre = (dot(state, w_node_s[...]) + dot(agg, w_agg_s[...])) * 0.5
        hidden = (pre + pre * jnp.tanh(pre)).astype(BF16)
        out = dot(hidden, w_out_s[...])
        mean = jnp.mean(out, axis=-1, keepdims=True)
        centred = out - mean
        var = jnp.mean(centred * centred, axis=-1, keepdims=True)
        norm = centred * lax.rsqrt(var + 1e-05) * gain_ref[...]
        proc = (state.astype(F32) + norm).astype(BF16)
        proc_s[piece(c)] = proc
        store_proc(c).start()
        dec_s[some_nodes] = dot(proc, w_dec_s[...]).reshape(-1, members, LANES)

    for c in range(CHUNKS):
        update(c)

    tiles = fore_s.shape[0]
    some = tiles // CHUNKS

    def store_fore(c):
        span = pl.ds(c * some, some)
        return pltpu.make_async_copy(fore_s.at[span], fore_hbm.at[span], out_sem.at[CHUNKS + c])

    for c in range(CHUNKS):

        def spread(pair, carry):
            back = back_s[:, pl.ds(pl.multiple_of(pair * 2 * GROUP, 2 * GROUP), 2 * GROUP), :]
            back = jnp.swapaxes(back.astype(F32), 0, 1).reshape(2 * tile, LANES)
            for i in range(2):
                t = pair * 2 + i
                parts = [dec_s[parent_ref[t * GROUP + q]] for q in range(GROUP)]
                values = jnp.concatenate(parts, axis=0) + back[i * tile : (i + 1) * tile]
                fore_s[t] = values.astype(BF16)
            return carry

        lax.fori_loop(c * some // 2, (c + 1) * some // 2, spread, 0, unroll=4)
        store_fore(c).start()

    for c in range(CHUNKS):
        store_proc(c).wait()
        store_fore(c).wait()


def forecast(projected, before, after, back, senders, parent, weights):
    latent, sent, recv = projected
    count, width = latent.shape
    members = back.shape[0]
    grid_rows = members * back.shape[1]
    rim = before.shape[0]
    tiles = lax.axis_size("member") * lax.axis_size("region")
    hbm = pl.BlockSpec(memory_space=pl.ANY)
    w_shape = pltpu.VMEM(weights[1].shape, BF16)
    return pl.pallas_call(
        forecast_kernel,
        out_shape=(
            jax.ShapeDtypeStruct((count, width), BF16),
            jax.ShapeDtypeStruct((tiles, grid_rows // tiles, LANES), BF16),
        ),
        in_specs=[SM, SM, hbm, hbm, hbm, VM, VM, hbm, VM, hbm, hbm, hbm, VM, hbm],
        out_specs=(hbm, hbm),
        scratch_shapes=[
            pltpu.VMEM(((count + 2 * rim) // MEMBERS, width // LANES, MEMBERS, LANES), F32),
            pltpu.VMEM((count // MEMBERS, width // LANES, MEMBERS, LANES), F32),
            pltpu.VMEM((count // MEMBERS, MEMBERS, LANES), F32),
            pltpu.VMEM((count, width), BF16),
            pltpu.VMEM((count, width), BF16),
            pltpu.VMEM(back.shape, BF16),
            pltpu.VMEM((count, width), BF16),
            pltpu.VMEM((tiles, grid_rows // tiles, LANES), BF16),
            w_shape,
            w_shape,
            w_shape,
            pltpu.VMEM(weights[5].shape, BF16),
            pltpu.SemaphoreType.DMA((2 * CHUNKS + 6,)),
            pltpu.SemaphoreType.DMA((2 * CHUNKS,)),
        ],
        compiler_params=pltpu.CompilerParams(vmem_limit_bytes=56 * 2**20),
        name="forecast",
    )(senders.reshape(-1), parent, latent, sent, recv, before, after, back, *weights)


def point_rows(ens_ref, region, start):
    size = 8
    blocks = [
        ens_ref[g, region, pl.ds(start, 2 * size), :].astype(F32) for g in range(ens_ref.shape[0])
    ]
    return [
        jnp.concatenate([b[i * size : (i + 1) * size] for b in blocks], axis=0) for i in range(2)
    ]


def observe_kernel(count_ref, loc_ref, ens_ref, value_ref, var_ref, pay_ref):
    groups, regions, rows, _ = ens_ref.shape
    size = 8
    members = groups * size
    slots = loc_ref.shape[1]
    pairs = size // 2
    loc = loc_ref[...]
    flat = loc % LANES * LANES + loc // LANES
    entry = lax.broadcasted_iota(jnp.int32, (2 * LANES, slots), 0)

    def add(pair, acc):
        start = pl.multiple_of(pair % pairs * 2 * size, 2 * size)
        state = jnp.concatenate(point_rows(ens_ref, pair // pairs, start), axis=1).astype(BF16)
        chosen = jnp.where(entry == flat - pair * 2 * LANES, 1.0, 0.0).astype(BF16)
        return acc + dot(state, chosen)

    yens = lax.fori_loop(0, regions * pairs, add, jnp.zeros((members, slots), F32), unroll=8)
    ybar = jnp.mean(yens, axis=0, keepdims=True)
    slot = lax.broadcasted_iota(jnp.int32, (1, slots), 1)
    rinv = jnp.where(slot < count_ref[0], 1.0, 0.0) / var_ref[...]
    dres = (value_ref[...] - ybar) * rinv
    row = lax.broadcasted_iota(jnp.int32, (16, slots), 0)
    extra = jnp.where(row == 0, rinv, jnp.where(row == 1, dres, 0.0))
    pay_ref[0:members] = (yens - ybar).astype(BF16)
    pay_ref[members : members + 16] = extra.astype(BF16)


def observe(ens, loc, count, value, var):
    groups, regions, rows, _ = ens.shape
    return pl.pallas_call(
        observe_kernel,
        out_shape=jax.ShapeDtypeStruct((groups * 8 + 16, loc.shape[0]), BF16),
        in_specs=[SM, VM, VM, VM, VM],
        out_specs=VM,
        compiler_params=pltpu.CompilerParams(vmem_limit_bytes=40 * 2**20),
        name="observe",
    )(count, loc[None], ens, value[None], var[None])


def analyse_kernel(
    before_ref,
    own_ref,
    after_ref,
    nbr_ref,
    loc_ref,
    ens_hbm,
    inc_hbm,
    ens_ref,
    inc_ref,
    pay_s,
    bl_s,
    bk_s,
    g_s,
    m_s,
    r_s,
    q_s,
    t_s,
    c_s,
    w_s,
    in_sem,
    out_sem,
):
    groups, regions, rows, _ = ens_ref.shape
    load = pltpu.make_async_copy(ens_hbm, ens_ref, in_sem.at[0])
    load.start()
    size = 8
    members = groups * size
    order = nbr_ref.shape[0]
    nb = order // size
    slots = own_ref.shape[1]
    sub = lax.broadcasted_iota(jnp.int32, (size, LANES), 0)

    for i, ref in enumerate((before_ref, own_ref, after_ref)):
        pay_s[:, i * slots : (i + 1) * slots] = ref[...]

    def full(row):
        return jnp.broadcast_to(row, (size, LANES))

    entry = lax.broadcasted_iota(jnp.int32, (3 * slots, 2 * LANES), 0)

    def gather(step, vec):
        index = jnp.concatenate(
            [nbr_ref[pl.ds(2 * step, 1), :], nbr_ref[pl.ds(2 * step + 1, 1), :]], axis=1
        )
        chosen = jnp.where(entry == index, 1.0, 0.0).astype(BF16)
        both = dot(pay_s[...], chosen)
        vec = list(vec)
        for i in range(2):
            l = 2 * step + i
            panel = both[:, i * LANES : (i + 1) * LANES]
            weight = loc_ref[pl.ds(l, 1), :]
            root = jnp.sqrt(weight * panel[members : members + 1])
            dl = weight * panel[members + 1 : members + 2]
            for g in range(groups):
                yl = panel[g * size : (g + 1) * size]
                vec[g] = vec[g] + yl * dl
                b = yl * root
                bl_s[pl.ds(pl.multiple_of(l * members + g * size, size), size), :] = b
                bk_s[pl.ds(g * size * order + l, size, stride=order), :] = b
        return tuple(vec)

    zero = jnp.zeros((size, LANES), F32)
    vec = lax.fori_loop(0, order // 2, gather, tuple([zero] * groups), unroll=2)

    def row_of(ref, r):
        return jnp.broadcast_to(ref[pl.ds(r, 1), :], (size, LANES))

    def accumulate(start, stop, left_row, right, a, acc):
        width = nb - a

        def body(k, acc):
            rhs = [
                right[pl.ds(pl.multiple_of(k * order + (a + j) * size, size), size), :]
                for j in range(width)
            ]
            out = []
            for i in range(size):
                lhs = left_row(k, i)
                for j in range(width):
                    out.append(acc[i * width + j] + lhs * rhs[j])
            return tuple(out)

        return lax.fori_loop(start, stop, body, acc, unroll=UNROLL)

    def finish_group(a, acc, finish):
        width = nb - a
        for i in range(size):
            for j in range(width):
                finish(a * size + i, a + j, acc[i * width + j])

    def gram(ref, count, finish):
        for a in range(nb):
            acc = accumulate(
                0,
                count,
                lambda k, i: row_of(ref, k * order + a * size + i),
                ref,
                a,
                tuple([zero] * (size * (nb - a))),
            )
            finish_group(a, acc, finish)

    def product(left, right, finish):
        for a in range(nb):
            edge = (a + 1) * size
            acc = accumulate(
                0,
                edge,
                lambda k, i: row_of(left, k * order + a * size + i),
                right,
                a,
                tuple([zero] * (size * (nb - a))),
            )
            if edge < order:
                acc = accumulate(
                    edge,
                    order,
                    lambda k, i: row_of(left, (a * size + i) * order + k),
                    right,
                    a,
                    acc,
                )
            finish_group(a, acc, finish)

    def at(ref, i, jb):
        return ref[pl.ds(i * order + jb * size, size), :]

    def put(ref, i, jb, value):
        ref[pl.ds(i * order + jb * size, size), :] = value
        if jb != i // size:
            ref[pl.ds(jb * size * order + i, size, stride=order), :] = value

    def upper(ref, i, jb, value):
        ref[pl.ds(i * order + jb * size, size), :] = value

    blocks = [(i, jb) for i in range(order) for jb in range(i // size, nb)]
    gram(bk_s, members, functools.partial(upper, g_s))

    square, cross, trace = zero, zero, zero
    for i, jb in blocks:
        g = at(g_s, i, jb)
        if jb == i // size:
            square = square + g * g
            trace = trace + jnp.where(sub == i % size, g, 0.0)
        else:
            cross = cross + g * g
    square = square + 2.0 * cross
    base = members - 1.0
    total = (
        base * base * members
        + 2.0 * base * jnp.sum(trace, axis=0, keepdims=True)
        + jnp.sum(square, axis=0, keepdims=True)
    )
    scale = jnp.sqrt(total)
    inv = 1.0 / scale
    a_coef = full(base * inv)

    z = 1.5 - 0.5 * a_coef
    for i, jb in blocks:
        g = at(g_s, i, jb) * inv
        put(g_s, i, jb, g)
        m, r = zero, -0.5 * g
        if jb == i // size:
            here = sub == i % size
            m = jnp.where(here, -0.5, 0.0)
            r = r + jnp.where(here, z, 0.0)
        upper(m_s, i, jb, m)
        put(r_s, i, jb, r)
        upper(q_s, i, jb, a_coef * m + r)

    for it in range(1, NS_ITERS):
        last = it == NS_ITERS - 1
        t = 1.5 - 0.5 * a_coef * z * z

        def tmat(i, jb, v):
            upper(t_s, i, jb, -0.5 * (v + z * (at(q_s, i, jb) - at(r_s, i, jb))))

        product(q_s, r_s, tmat)

        def mmat(i, jb, v):
            m = t * at(m_s, i, jb) + v
            if last:
                put(m_s, i, jb, m * inv)
            else:
                upper(m_s, i, jb, m)

        product(t_s, r_s, mmat)
        z = t * z
        if not last:

            def rmat(i, jb, v):
                if jb == i // size:
                    v = v + jnp.where(sub == i % size, z, 0.0)
                put(r_s, i, jb, v)
                upper(q_s, i, jb, a_coef * at(m_s, i, jb) + v)

            product(m_s, g_s, rmat)

    root = full(lax.rsqrt(scale))

    def cmat(step, carry):
        for g0 in range(0, groups, 4):
            acc = [zero] * 16
            for k in range(order):
                b = [bl_s[pl.ds(k * members + (g0 + g) * size, size), :] for g in range(4)]
                for i in range(4):
                    lhs = row_of(m_s, k * order + step * 4 + i)
                    for g in range(4):
                        acc[i * 4 + g] = acc[i * 4 + g] + lhs * b[g]
            for i in range(4):
                for g in range(4):
                    start = (step * 4 + i) * members + (g0 + g) * size
                    c_s[pl.ds(pl.multiple_of(start, size), size), :] = acc[i * 4 + g]
        return carry

    lax.fori_loop(0, order // 4, cmat, 0)

    def smat_times(vector):
        for g in range(groups):
            t_s[pl.ds(g * size, size), :] = vector[g]
        down = [zero] * nb
        for k in range(members):
            v = row_of(t_s, k)
            for j in range(nb):
                down[j] = down[j] + v * bk_s[pl.ds(k * order + j * size, size), :]
        for j in range(nb):
            t_s[pl.ds(members + j * size, size), :] = down[j]
        up = [z * vector[g] for g in range(groups)]
        for l in range(order):
            u = row_of(t_s, members + l)
            for g in range(groups):
                up[g] = up[g] + u * c_s[pl.ds(l * members + g * size, size), :]
        return [root * up[g] for g in range(groups)]

    wbar = smat_times(smat_times(vec))
    for g in range(groups):
        t_s[pl.ds(g * size, size), :] = wbar[g]

    gain = full(jnp.float32(base) ** 0.5 * root)

    half = members // 2

    def vmat(step, carry):
        ks = [2 * step, 2 * step + 1, half + 2 * step, half + 2 * step + 1]
        slabs = [[], [], [], []]
        for g0 in range(0, groups, 4):
            acc = [zero] * 16
            for l in range(order):
                c = [c_s[pl.ds(l * members + (g0 + g) * size, size), :] for g in range(4)]
                for i in range(4):
                    lhs = row_of(bk_s, ks[i] * order + l)
                    for g in range(4):
                        acc[i * 4 + g] = acc[i * 4 + g] + lhs * c[g]
            for i in range(4):
                for g in range(4):
                    here = sub + (g0 + g) * size == ks[i]
                    s = gain * (acc[i * 4 + g] + jnp.where(here, z, 0.0))
                    s = s + t_s[pl.ds((g0 + g) * size, size), :]
                    slabs[i].append(s - jnp.where(here, 1.0, 0.0))
        for i in range(2):
            both = jnp.concatenate(slabs[i] + slabs[2 + i], axis=0)
            start = pl.multiple_of(ks[i] * LANES, LANES)
            w_s[pl.ds(start, LANES), :] = jnp.transpose(both)
        return carry

    lax.fori_loop(0, half // 2, vmat, 0)
    load.wait()

    def apply(pair, carry):
        region, place = pair // (size // 2), pair % (size // 2)
        start = pl.multiple_of(place * 2 * size, 2 * size)
        outs = []
        for second, x in enumerate(point_rows(ens_ref, region, start)):
            x = (x - jnp.mean(x, axis=0, keepdims=True)).astype(BF16)
            gap = jnp.zeros_like(x)
            rhs = jnp.concatenate(
                [jnp.concatenate([x, gap], axis=1), jnp.concatenate([gap, x], axis=1)], axis=0
            )
            lhs = w_s[pl.ds(pair * 2 + second, half, stride=LANES), :].astype(BF16)
            outs.append(dot(lhs, rhs))
        for g in range(groups):
            top, side = g * size % half, g * size // half
            piece = [
                o[top : top + size, side * LANES : (side + 1) * LANES] for o in outs
            ]
            inc_ref[g, region, pl.ds(start, 2 * size), :] = jnp.concatenate(
                piece, axis=0
            ).astype(BF16)
        return carry

    steps = 4
    some = regions // steps
    stores = []
    for c in range(steps):
        lax.fori_loop(c * some * size // 2, (c + 1) * some * size // 2, apply, 0, unroll=8)
        span = pl.ds(c * some, some)
        stores.append(
            pltpu.make_async_copy(inc_ref.at[:, span], inc_hbm.at[:, span], out_sem.at[c])
        )
        stores[c].start()
    for copy in stores:
        copy.wait()


def analyse(before, own, after, nbr, loc, ens):
    order, points = nbr.shape
    members = ens.shape[0] * 8
    hbm = pl.BlockSpec(memory_space=pl.ANY)
    small = pltpu.VMEM((order * order, LANES), F32)
    tall = pltpu.VMEM((order * members, LANES), F32)
    return pl.pallas_call(
        analyse_kernel,
        out_shape=jax.ShapeDtypeStruct(ens.shape, BF16),
        in_specs=[VM] * 5 + [hbm],
        out_specs=hbm,
        scratch_shapes=[
            pltpu.VMEM(ens.shape, BF16),
            pltpu.VMEM(ens.shape, BF16),
            pltpu.VMEM((members + 16, 3 * own.shape[1]), BF16),
            tall,
            tall,
            small,
            small,
            small,
            small,
            small,
            tall,
            pltpu.VMEM((members // 2 * LANES, LANES), F32),
            pltpu.SemaphoreType.DMA((1,)),
            pltpu.SemaphoreType.DMA((4,)),
        ],
        compiler_params=pltpu.CompilerParams(vmem_limit_bytes=56 * 2**20),
        name="analyse",
    )(before, own, after, nbr, loc, ens)


def finish_kernel(fore_hbm, inc_hbm, out_hbm, fore_s, inc_s, out_s, in_sem, out_sem):
    members, grid_r, _ = out_s.shape
    tiles, rows, _ = fore_s.shape
    steps = in_sem.shape[0] // 2
    some, points = tiles // steps, grid_r // steps

    def loads(c):
        span = pl.ds(c * some, some)
        return [
            pltpu.make_async_copy(fore_hbm.at[span], fore_s.at[span], in_sem.at[c]),
            pltpu.make_async_copy(inc_hbm.at[span], inc_s.at[span], in_sem.at[steps + c]),
        ]

    def store(c):
        span = pl.ds(c * points, points)
        return pltpu.make_async_copy(out_s.at[:, span], out_hbm.at[:, span], out_sem.at[c])

    for c in range(steps):
        for copy in loads(c):
            copy.start()
    for c in range(steps):
        for copy in loads(c):
            copy.wait()
        span = pl.ds(c * some, some)
        total = fore_s[span].astype(F32) + inc_s[span].astype(F32)
        total = jnp.swapaxes(total.reshape(points, members, LANES), 0, 1)
        out_s[:, pl.ds(c * points, points), :] = total.astype(BF16)
        store(c).start()
    for c in range(steps):
        store(c).wait()


def finish(fore, inc, members):
    tiles, rows, _ = fore.shape
    shape = (members, tiles * rows // members, LANES)
    steps = 8
    hbm = pl.BlockSpec(memory_space=pl.ANY)
    return pl.pallas_call(
        finish_kernel,
        out_shape=jax.ShapeDtypeStruct(shape, BF16),
        in_specs=[hbm, hbm],
        out_specs=hbm,
        scratch_shapes=[
            pltpu.VMEM(fore.shape, BF16),
            pltpu.VMEM(fore.shape, BF16),
            pltpu.VMEM(shape, BF16),
            pltpu.SemaphoreType.DMA((2 * steps,)),
            pltpu.SemaphoreType.DMA((steps,)),
        ],
        compiler_params=pltpu.CompilerParams(vmem_limit_bytes=40 * 2**20),
        name="finish",
    )(fore, inc)


def neighbours(inner, outer, axis, wrap):
    count = lax.axis_size(axis)
    within = [(i, i ^ 1) for i in range(count)]
    links = [(i, (i + 1) % count) for i in range(1, count if wrap else count - 1, 2)]
    across = links + [(b, a) for a, b in links]
    got = lax.ppermute(outer, axis, across)
    return lax.ppermute(inner, axis, within), got


def swapped(index, low, high, odd):
    moved = jnp.where(index < low, index + high, jnp.where(index >= high, index - high, index))
    return jnp.where(odd == 1, moved, index)


def exchange(blocks):
    return lax.all_to_all(blocks, MR, split_axis=0, concat_axis=0, tiled=True)


def shards(
    latent_vertex_values,
    background_field,
    edge_senders,
    grid_parent,
    w_send,
    w_recv,
    w_node,
    w_agg,
    w_out,
    norm_gain,
    w_dec,
    obs_loc,
    obs_count,
    obs_value,
    obs_var,
    obs_nbr,
    loc_weight,
):
    members, nodes, width = latent_vertex_values.shape
    grid_r = background_field.shape[1]
    groups, regions = lax.axis_size("member"), lax.axis_size("region")

    def node_major(array):
        return array.transpose(1, 0, 2).reshape(-1, array.shape[2])

    odd = lax.axis_index("region") % 2

    def rim(start):
        return node_major(lax.dynamic_slice_in_dim(latent_vertex_values, start, RIM, 1))

    inner, outer = neighbours(
        rim(jnp.where(odd == 1, 0, nodes - RIM)),
        rim(jnp.where(odd == 1, nodes - RIM, 0)),
        "region",
        True,
    )
    edges = swapped(edge_senders - (nodes - RIM), RIM, nodes + RIM, odd)
    weights = (w_send, w_node, w_agg, w_out, norm_gain[None], w_dec)
    processed, fore = forecast(
        project(latent_vertex_values, w_send, w_recv),
        outer,
        inner,
        background_field,
        edges,
        grid_parent,
        weights,
    )
    processed = processed.reshape(nodes, members, width).transpose(1, 0, 2)
    ens = exchange(fore)
    ens = ens.reshape(groups, regions, *ens.shape[1:])
    payload = observe(ens, obs_loc, obs_count, obs_value, obs_var)
    pay_inner, pay_outer = neighbours(payload, payload, MR, False)
    slots = obs_loc.shape[0]
    nbr = swapped(obs_nbr, slots, 2 * slots, odd)
    inc = analyse(pay_outer, payload, pay_inner, nbr, loc_weight, ens)
    landed = exchange(inc.reshape(groups * regions, *inc.shape[2:]))
    return processed, finish(fore, landed, members)


def solution(mesh):
    in_specs = (
        P("member", "region", None),
        P("member", "region", None),
        P("region", None),
        P("region"),
        P(),
        P(),
        P(),
        P(),
        P(),
        P(),
        P(),
        P(MR),
        P(MR),
        P(MR),
        P(MR),
        P(None, MR),
        P(None, MR),
    )
    out_specs = (P("member", "region", None), P("member", "region", None))
    return jax.shard_map(shards, mesh=mesh, in_specs=in_specs, out_specs=out_specs, check_vma=False)
```

```python
import functools

import jax
import jax.numpy as jnp
from jax import lax
from jax.experimental import pallas as pl
from jax.experimental.pallas import tpu as pltpu
from jax.sharding import PartitionSpec as P

NS_ITERS = 6
LANES = 128
RIM = 64
MEMBERS = 8
GROUP = 8
CHUNKS = 4
UNROLL = 8
F32 = jnp.float32
BF16 = jnp.bfloat16
MR = ("member", "region")
VM = pl.BlockSpec(memory_space=pltpu.VMEM)
SM = pl.BlockSpec(memory_space=pltpu.SMEM)


def dot(a, b):
    return jnp.dot(a, b, preferred_element_type=F32)


def lane_blocks(ref, first, values):
    for c in range(values.shape[1] // LANES):
        part = values[:, c * LANES : (c + 1) * LANES].reshape(-1, MEMBERS, LANES)
        ref[first // MEMBERS : first // MEMBERS + part.shape[0], c] = part


def project_kernel(
    latent_hbm,
    w_send_ref,
    w_recv_ref,
    state_hbm,
    send_hbm,
    recv_hbm,
    raw_s,
    state_s,
    send_s,
    recv_s,
    in_sem,
    out_sem,
):
    members, nodes, width = latent_hbm.shape
    some = nodes // CHUNKS
    rows = members * some

    def own(c):
        return pl.ds(c * some, some)

    def piece(c):
        return pl.ds(c * rows, rows)

    loads = [
        pltpu.make_async_copy(latent_hbm.at[:, own(c)], raw_s.at[:, own(c)], in_sem.at[c])
        for c in range(CHUNKS)
    ]
    for copy in loads:
        copy.start()
    stores = []
    for c in range(CHUNKS):
        loads[c].wait()
        turned = jnp.swapaxes(raw_s[:, own(c)].astype(F32), 0, 1)
        state = turned.reshape(rows, width).astype(BF16)
        state_s[piece(c)] = state
        send_s[piece(c)] = dot(state, w_send_ref[...]).astype(BF16)
        lane_blocks(recv_s, c * rows, dot(state, w_recv_ref[...]) * 0.5)
        pairs = [
            (state_s.at[piece(c)], state_hbm.at[piece(c)]),
            (send_s.at[piece(c)], send_hbm.at[piece(c)]),
            (recv_s.at[own(c)], recv_hbm.at[own(c)]),
        ]
        for k, (src, dst) in enumerate(pairs):
            copy = pltpu.make_async_copy(src, dst, out_sem.at[3 * c + k])
            copy.start()
            stores.append(copy)
    for copy in stores:
        copy.wait()


def project(latent, w_send, w_recv):
    members, nodes, width = latent.shape
    count = members * nodes
    flat = (count, width)
    blocks = (nodes, width // LANES, members, LANES)
    hbm = pl.BlockSpec(memory_space=pl.ANY)
    return pl.pallas_call(
        project_kernel,
        out_shape=(
            jax.ShapeDtypeStruct(flat, BF16),
            jax.ShapeDtypeStruct(flat, BF16),
            jax.ShapeDtypeStruct(blocks, F32),
        ),
        in_specs=[hbm, VM, VM],
        out_specs=(hbm, hbm, hbm),
        scratch_shapes=[
            pltpu.VMEM(latent.shape, BF16),
            pltpu.VMEM(flat, BF16),
            pltpu.VMEM(flat, BF16),
            pltpu.VMEM(blocks, F32),
            pltpu.SemaphoreType.DMA((CHUNKS,)),
            pltpu.SemaphoreType.DMA((3 * CHUNKS,)),
        ],
        compiler_params=pltpu.CompilerParams(vmem_limit_bytes=61 * 2**20),
        cost_estimate=pl.CostEstimate(
            flops=4 * count * width * width, bytes_accessed=10 * count * width, transcendentals=0
        ),
        name="project",
    )(latent, w_send, w_recv)


def forecast_kernel(
    edge_ref,
    parent_ref,
    latent_hbm,
    sent_hbm,
    recv_hbm,
    before_ref,
    after_ref,
    back_hbm,
    w_send_hbm,
    w_node_hbm,
    w_agg_hbm,
    w_out_hbm,
    gain_ref,
    w_dec_hbm,
    proc_hbm,
    fore_hbm,
    send_s,
    recv_s,
    dec_s,
    sent_s,
    latent_s,
    back_s,
    proc_s,
    fore_s,
    w_send_s,
    w_node_s,
    w_agg_s,
    w_out_s,
    w_dec_s,
    in_sem,
    out_sem,
):
    nodes, cols, members, _ = recv_hbm.shape
    count, width = latent_hbm.shape
    rim = before_ref.shape[0]
    degree = edge_ref.shape[0] // nodes
    rows = count // CHUNKS
    tile = members * GROUP

    def piece(c):
        return pl.ds(c * rows, rows)

    def own(c):
        return pl.ds(c * (nodes // CHUNKS), nodes // CHUNKS)

    sent = [
        pltpu.make_async_copy(sent_hbm.at[piece(c)], sent_s.at[piece(c)], in_sem.at[c])
        for c in range(CHUNKS)
    ]
    mine = [
        pltpu.make_async_copy(recv_hbm.at[own(c)], recv_s.at[own(c)], in_sem.at[CHUNKS + c])
        for c in range(CHUNKS)
    ]
    later = [
        pltpu.make_async_copy(src, dst, in_sem.at[2 * CHUNKS + i])
        for i, (src, dst) in enumerate(
            [
                (latent_hbm, latent_s),
                (w_node_hbm, w_node_s),
                (w_agg_hbm, w_agg_s),
                (w_out_hbm, w_out_s),
                (w_dec_hbm, w_dec_s),
                (back_hbm, back_s),
            ]
        )
    ]
    first = pltpu.make_async_copy(w_send_hbm, w_send_s, in_sem.at[2 * CHUNKS + 6])
    for copy in sent + [first] + mine + later:
        copy.start()

    def rim_of(state):
        return dot(state, w_send_s[...]).astype(BF16).astype(F32) * 0.5

    for c in range(CHUNKS):
        sent[c].wait()
        lane_blocks(send_s, rim + c * rows, sent_s[piece(c)].astype(F32) * 0.5)
    first.wait()
    lane_blocks(send_s, 0, rim_of(before_ref[...]))
    lane_blocks(send_s, rim + count, rim_of(after_ref[...]))

    def aggregate(n, carry):
        mine = recv_s[n]
        total = jnp.zeros_like(mine)
        for e in range(degree):
            half = send_s[edge_ref[n * degree + e]] + mine
            total = total + (half + half * jnp.tanh(half))
        recv_s[n] = total
        return carry

    for c in range(CHUNKS):
        mine[c].wait()
        lax.fori_loop(c * nodes // CHUNKS, (c + 1) * nodes // CHUNKS, aggregate, 0, unroll=8)
    for copy in later:
        copy.wait()

    def store_proc(c):
        return pltpu.make_async_copy(proc_s.at[piece(c)], proc_hbm.at[piece(c)], out_sem.at[c])

    def update(c):
        state = latent_s[piece(c)]
        some_nodes = pl.ds(c * (rows // members), rows // members)
        agg = jnp.concatenate(
            [recv_s[some_nodes, i].reshape(rows, LANES) for i in range(cols)], axis=1
        ).astype(BF16)
        pre = (dot(state, w_node_s[...]) + dot(agg, w_agg_s[...])) * 0.5
        hidden = (pre + pre * jnp.tanh(pre)).astype(BF16)
        out = dot(hidden, w_out_s[...])
        mean = jnp.mean(out, axis=-1, keepdims=True)
        centred = out - mean
        var = jnp.mean(centred * centred, axis=-1, keepdims=True)
        norm = centred * lax.rsqrt(var + 1e-05) * gain_ref[...]
        proc = (state.astype(F32) + norm).astype(BF16)
        proc_s[piece(c)] = proc
        store_proc(c).start()
        dec_s[some_nodes] = dot(proc, w_dec_s[...]).reshape(-1, members, LANES)

    for c in range(CHUNKS):
        update(c)

    tiles = fore_s.shape[0]
    some = tiles // CHUNKS

    def store_fore(c):
        span = pl.ds(c * some, some)
        return pltpu.make_async_copy(fore_s.at[span], fore_hbm.at[span], out_sem.at[CHUNKS + c])

    for c in range(CHUNKS):

        def spread(pair, carry):
            back = back_s[:, pl.ds(pl.multiple_of(pair * 2 * GROUP, 2 * GROUP), 2 * GROUP), :]
            back = jnp.swapaxes(back.astype(F32), 0, 1).reshape(2 * tile, LANES)
            for i in range(2):
                t = pair * 2 + i
                parts = [dec_s[parent_ref[t * GROUP + q]] for q in range(GROUP)]
                values = jnp.concatenate(parts, axis=0) + back[i * tile : (i + 1) * tile]
                fore_s[t] = values.astype(BF16)
            return carry

        lax.fori_loop(c * some // 2, (c + 1) * some // 2, spread, 0, unroll=4)
        store_fore(c).start()

    for c in range(CHUNKS):
        store_proc(c).wait()
        store_fore(c).wait()


def forecast(projected, before, after, back, senders, parent, weights):
    latent, sent, recv = projected
    count, width = latent.shape
    members = back.shape[0]
    grid_rows = members * back.shape[1]
    rim = before.shape[0]
    tiles = lax.axis_size("member") * lax.axis_size("region")
    hbm = pl.BlockSpec(memory_space=pl.ANY)
    w_shape = pltpu.VMEM(weights[1].shape, BF16)
    return pl.pallas_call(
        forecast_kernel,
        out_shape=(
            jax.ShapeDtypeStruct((count, width), BF16),
            jax.ShapeDtypeStruct((tiles, grid_rows // tiles, LANES), BF16),
        ),
        in_specs=[SM, SM, hbm, hbm, hbm, VM, VM, hbm, hbm, hbm, hbm, hbm, VM, hbm],
        out_specs=(hbm, hbm),
        scratch_shapes=[
            pltpu.VMEM(((count + 2 * rim) // MEMBERS, width // LANES, MEMBERS, LANES), F32),
            pltpu.VMEM((count // MEMBERS, width // LANES, MEMBERS, LANES), F32),
            pltpu.VMEM((count // MEMBERS, MEMBERS, LANES), F32),
            pltpu.VMEM((count, width), BF16),
            pltpu.VMEM((count, width), BF16),
            pltpu.VMEM(back.shape, BF16),
            pltpu.VMEM((count, width), BF16),
            pltpu.VMEM((tiles, grid_rows // tiles, LANES), BF16),
            w_shape,
            w_shape,
            w_shape,
            w_shape,
            pltpu.VMEM(weights[5].shape, BF16),
            pltpu.SemaphoreType.DMA((2 * CHUNKS + 7,)),
            pltpu.SemaphoreType.DMA((2 * CHUNKS,)),
        ],
        compiler_params=pltpu.CompilerParams(vmem_limit_bytes=60 * 2**20),
        name="forecast",
    )(senders.reshape(-1), parent, latent, sent, recv, before, after, back, *weights)


def point_rows(ens_ref, region, start):
    size = 8
    blocks = [
        ens_ref[g, region, pl.ds(start, 2 * size), :].astype(F32) for g in range(ens_ref.shape[0])
    ]
    return [
        jnp.concatenate([b[i * size : (i + 1) * size] for b in blocks], axis=0) for i in range(2)
    ]


def observe_kernel(count_ref, loc_ref, ens_ref, value_ref, var_ref, pay_ref):
    groups, regions, rows, _ = ens_ref.shape
    size = 8
    members = groups * size
    slots = loc_ref.shape[1]
    pairs = size // 2
    loc = loc_ref[...]
    flat = loc % LANES * LANES + loc // LANES
    entry = lax.broadcasted_iota(jnp.int32, (2 * LANES, slots), 0)

    def add(pair, acc):
        start = pl.multiple_of(pair % pairs * 2 * size, 2 * size)
        state = jnp.concatenate(point_rows(ens_ref, pair // pairs, start), axis=1).astype(BF16)
        chosen = jnp.where(entry == flat - pair * 2 * LANES, 1.0, 0.0).astype(BF16)
        return acc + dot(state, chosen)

    yens = lax.fori_loop(0, regions * pairs, add, jnp.zeros((members, slots), F32), unroll=8)
    ybar = jnp.mean(yens, axis=0, keepdims=True)
    slot = lax.broadcasted_iota(jnp.int32, (1, slots), 1)
    rinv = jnp.where(slot < count_ref[0], 1.0, 0.0) / var_ref[...]
    dres = (value_ref[...] - ybar) * rinv
    row = lax.broadcasted_iota(jnp.int32, (16, slots), 0)
    extra = jnp.where(row == 0, rinv, jnp.where(row == 1, dres, 0.0))
    pay_ref[0:members] = (yens - ybar).astype(BF16)
    pay_ref[members : members + 16] = extra.astype(BF16)


def observe(ens, loc, count, value, var):
    groups, regions, rows, _ = ens.shape
    return pl.pallas_call(
        observe_kernel,
        out_shape=jax.ShapeDtypeStruct((groups * 8 + 16, loc.shape[0]), BF16),
        in_specs=[SM, VM, VM, VM, VM],
        out_specs=VM,
        compiler_params=pltpu.CompilerParams(vmem_limit_bytes=40 * 2**20),
        name="observe",
    )(count, loc[None], ens, value[None], var[None])


def analyse_kernel(
    before_ref,
    own_ref,
    after_ref,
    nbr_ref,
    loc_ref,
    ens_hbm,
    inc_hbm,
    ens_ref,
    inc_ref,
    pay_s,
    bl_s,
    bk_s,
    g_s,
    m_s,
    r_s,
    q_s,
    t_s,
    c_s,
    w_s,
    in_sem,
    out_sem,
):
    groups, regions, rows, _ = ens_ref.shape
    load = pltpu.make_async_copy(ens_hbm, ens_ref, in_sem.at[0])
    load.start()
    size = 8
    members = groups * size
    order = nbr_ref.shape[0]
    nb = order // size
    slots = own_ref.shape[1]
    sub = lax.broadcasted_iota(jnp.int32, (size, LANES), 0)

    for i, ref in enumerate((before_ref, own_ref, after_ref)):
        pay_s[:, i * slots : (i + 1) * slots] = ref[...]

    def full(row):
        return jnp.broadcast_to(row, (size, LANES))

    entry = lax.broadcasted_iota(jnp.int32, (3 * slots, 2 * LANES), 0)

    def gather(step, vec):
        index = jnp.concatenate(
            [nbr_ref[pl.ds(2 * step, 1), :], nbr_ref[pl.ds(2 * step + 1, 1), :]], axis=1
        )
        chosen = jnp.where(entry == index, 1.0, 0.0).astype(BF16)
        both = dot(pay_s[...], chosen)
        vec = list(vec)
        for i in range(2):
            l = 2 * step + i
            panel = both[:, i * LANES : (i + 1) * LANES]
            weight = loc_ref[pl.ds(l, 1), :]
            root = jnp.sqrt(weight * panel[members : members + 1])
            dl = weight * panel[members + 1 : members + 2]
            for g in range(groups):
                yl = panel[g * size : (g + 1) * size]
                vec[g] = vec[g] + yl * dl
                b = yl * root
                bl_s[pl.ds(pl.multiple_of(l * members + g * size, size), size), :] = b
                bk_s[pl.ds(g * size * order + l, size, stride=order), :] = b
        return tuple(vec)

    zero = jnp.zeros((size, LANES), F32)
    vec = lax.fori_loop(0, order // 2, gather, tuple([zero] * groups), unroll=2)

    def row_of(ref, r):
        return jnp.broadcast_to(ref[pl.ds(r, 1), :], (size, LANES))

    def accumulate(start, stop, left_row, right, a, acc):
        width = nb - a

        def body(k, acc):
            rhs = [
                right[pl.ds(pl.multiple_of(k * order + (a + j) * size, size), size), :]
                for j in range(width)
            ]
            out = []
            for i in range(size):
                lhs = left_row(k, i)
                for j in range(width):
                    out.append(acc[i * width + j] + lhs * rhs[j])
            return tuple(out)

        return lax.fori_loop(start, stop, body, acc, unroll=UNROLL)

    def finish_group(a, acc, finish):
        width = nb - a
        for i in range(size):
            for j in range(width):
                finish(a * size + i, a + j, acc[i * width + j])

    def gram(ref, count, finish):
        for a in range(nb):
            acc = accumulate(
                0,
                count,
                lambda k, i: row_of(ref, k * order + a * size + i),
                ref,
                a,
                tuple([zero] * (size * (nb - a))),
            )
            finish_group(a, acc, finish)

    def product(left, right, finish):
        for a in range(nb):
            edge = (a + 1) * size
            acc = accumulate(
                0,
                edge,
                lambda k, i: row_of(left, k * order + a * size + i),
                right,
                a,
                tuple([zero] * (size * (nb - a))),
            )
            if edge < order:
                acc = accumulate(
                    edge,
                    order,
                    lambda k, i: row_of(left, (a * size + i) * order + k),
                    right,
                    a,
                    acc,
                )
            finish_group(a, acc, finish)

    def at(ref, i, jb):
        return ref[pl.ds(i * order + jb * size, size), :]

    def put(ref, i, jb, value):
        ref[pl.ds(i * order + jb * size, size), :] = value
        if jb != i // size:
            ref[pl.ds(jb * size * order + i, size, stride=order), :] = value

    def upper(ref, i, jb, value):
        ref[pl.ds(i * order + jb * size, size), :] = value

    blocks = [(i, jb) for i in range(order) for jb in range(i // size, nb)]
    gram(bk_s, members, functools.partial(upper, g_s))

    square, cross, trace = zero, zero, zero
    for i, jb in blocks:
        g = at(g_s, i, jb)
        if jb == i // size:
            square = square + g * g
            trace = trace + jnp.where(sub == i % size, g, 0.0)
        else:
            cross = cross + g * g
    square = square + 2.0 * cross
    base = members - 1.0
    total = (
        base * base * members
        + 2.0 * base * jnp.sum(trace, axis=0, keepdims=True)
        + jnp.sum(square, axis=0, keepdims=True)
    )
    scale = jnp.sqrt(total)
    inv = 1.0 / scale
    a_coef = full(base * inv)

    z = 1.5 - 0.5 * a_coef
    for i, jb in blocks:
        g = at(g_s, i, jb) * inv
        put(g_s, i, jb, g)
        m, r = zero, -0.5 * g
        if jb == i // size:
            here = sub == i % size
            m = jnp.where(here, -0.5, 0.0)
            r = r + jnp.where(here, z, 0.0)
        upper(m_s, i, jb, m)
        put(r_s, i, jb, r)
        upper(q_s, i, jb, a_coef * m + r)

    for it in range(1, NS_ITERS):
        last = it == NS_ITERS - 1
        t = 1.5 - 0.5 * a_coef * z * z

        def tmat(i, jb, v):
            upper(t_s, i, jb, -0.5 * (v + z * (at(q_s, i, jb) - at(r_s, i, jb))))

        product(q_s, r_s, tmat)

        def mmat(i, jb, v):
            m = t * at(m_s, i, jb) + v
            if last:
                put(m_s, i, jb, m * inv)
            else:
                upper(m_s, i, jb, m)

        product(t_s, r_s, mmat)
        z = t * z
        if not last:

            def rmat(i, jb, v):
                if jb == i // size:
                    v = v + jnp.where(sub == i % size, z, 0.0)
                put(r_s, i, jb, v)
                upper(q_s, i, jb, a_coef * at(m_s, i, jb) + v)

            product(m_s, g_s, rmat)

    root = full(lax.rsqrt(scale))

    def cmat(step, carry):
        for g0 in range(0, groups, 4):
            acc = [zero] * 16
            for k in range(order):
                b = [bl_s[pl.ds(k * members + (g0 + g) * size, size), :] for g in range(4)]
                for i in range(4):
                    lhs = row_of(m_s, k * order + step * 4 + i)
                    for g in range(4):
                        acc[i * 4 + g] = acc[i * 4 + g] + lhs * b[g]
            for i in range(4):
                for g in range(4):
                    start = (step * 4 + i) * members + (g0 + g) * size
                    c_s[pl.ds(pl.multiple_of(start, size), size), :] = acc[i * 4 + g]
        return carry

    lax.fori_loop(0, order // 4, cmat, 0)

    def smat_times(vector):
        for g in range(groups):
            t_s[pl.ds(g * size, size), :] = vector[g]
        down = [zero] * nb
        for k in range(members):
            v = row_of(t_s, k)
            for j in range(nb):
                down[j] = down[j] + v * bk_s[pl.ds(k * order + j * size, size), :]
        for j in range(nb):
            t_s[pl.ds(members + j * size, size), :] = down[j]
        up = [z * vector[g] for g in range(groups)]
        for l in range(order):
            u = row_of(t_s, members + l)
            for g in range(groups):
                up[g] = up[g] + u * c_s[pl.ds(l * members + g * size, size), :]
        return [root * up[g] for g in range(groups)]

    wbar = smat_times(smat_times(vec))
    for g in range(groups):
        t_s[pl.ds(g * size, size), :] = wbar[g]

    gain = full(jnp.float32(base) ** 0.5 * root)

    half = members // 2

    def vmat(step, carry):
        ks = [2 * step, 2 * step + 1, half + 2 * step, half + 2 * step + 1]
        slabs = [[], [], [], []]
        for g0 in range(0, groups, 4):
            acc = [zero] * 16
            for l in range(order):
                c = [c_s[pl.ds(l * members + (g0 + g) * size, size), :] for g in range(4)]
                for i in range(4):
                    lhs = row_of(bk_s, ks[i] * order + l)
                    for g in range(4):
                        acc[i * 4 + g] = acc[i * 4 + g] + lhs * c[g]
            for i in range(4):
                for g in range(4):
                    here = sub + (g0 + g) * size == ks[i]
                    s = gain * (acc[i * 4 + g] + jnp.where(here, z, 0.0))
                    s = s + t_s[pl.ds((g0 + g) * size, size), :]
                    slabs[i].append(s - jnp.where(here, 1.0, 0.0))
        for i in range(2):
            both = jnp.concatenate(slabs[i] + slabs[2 + i], axis=0)
            start = pl.multiple_of(ks[i] * LANES, LANES)
            w_s[pl.ds(start, LANES), :] = jnp.transpose(both)
        return carry

    lax.fori_loop(0, half // 2, vmat, 0)
    load.wait()

    def apply(pair, carry):
        region, place = pair // (size // 2), pair % (size // 2)
        start = pl.multiple_of(place * 2 * size, 2 * size)
        outs = []
        for second, x in enumerate(point_rows(ens_ref, region, start)):
            x = (x - jnp.mean(x, axis=0, keepdims=True)).astype(BF16)
            gap = jnp.zeros_like(x)
            rhs = jnp.concatenate(
                [jnp.concatenate([x, gap], axis=1), jnp.concatenate([gap, x], axis=1)], axis=0
            )
            lhs = w_s[pl.ds(pair * 2 + second, half, stride=LANES), :].astype(BF16)
            outs.append(dot(lhs, rhs))
        for g in range(groups):
            top, side = g * size % half, g * size // half
            piece = [
                o[top : top + size, side * LANES : (side + 1) * LANES] for o in outs
            ]
            inc_ref[g, region, pl.ds(start, 2 * size), :] = jnp.concatenate(
                piece, axis=0
            ).astype(BF16)
        return carry

    steps = 4
    some = regions // steps
    stores = []
    for c in range(steps):
        lax.fori_loop(c * some * size // 2, (c + 1) * some * size // 2, apply, 0, unroll=8)
        span = pl.ds(c * some, some)
        stores.append(
            pltpu.make_async_copy(inc_ref.at[:, span], inc_hbm.at[:, span], out_sem.at[c])
        )
        stores[c].start()
    for copy in stores:
        copy.wait()


def analyse(before, own, after, nbr, loc, ens):
    order, points = nbr.shape
    members = ens.shape[0] * 8
    hbm = pl.BlockSpec(memory_space=pl.ANY)
    small = pltpu.VMEM((order * order, LANES), F32)
    tall = pltpu.VMEM((order * members, LANES), F32)
    return pl.pallas_call(
        analyse_kernel,
        out_shape=jax.ShapeDtypeStruct(ens.shape, BF16),
        in_specs=[VM] * 5 + [hbm],
        out_specs=hbm,
        scratch_shapes=[
            pltpu.VMEM(ens.shape, BF16),
            pltpu.VMEM(ens.shape, BF16),
            pltpu.VMEM((members + 16, 3 * own.shape[1]), BF16),
            tall,
            tall,
            small,
            small,
            small,
            small,
            small,
            tall,
            pltpu.VMEM((members // 2 * LANES, LANES), F32),
            pltpu.SemaphoreType.DMA((1,)),
            pltpu.SemaphoreType.DMA((4,)),
        ],
        compiler_params=pltpu.CompilerParams(vmem_limit_bytes=56 * 2**20),
        name="analyse",
    )(before, own, after, nbr, loc, ens)


def finish_kernel(fore_hbm, inc_hbm, out_hbm, fore_s, inc_s, out_s, in_sem, out_sem):
    members, grid_r, _ = out_s.shape
    tiles, rows, _ = fore_s.shape
    steps = in_sem.shape[0] // 2
    some, points = tiles // steps, grid_r // steps

    def loads(c):
        span = pl.ds(c * some, some)
        return [
            pltpu.make_async_copy(fore_hbm.at[span], fore_s.at[span], in_sem.at[c]),
            pltpu.make_async_copy(inc_hbm.at[span], inc_s.at[span], in_sem.at[steps + c]),
        ]

    def store(c):
        span = pl.ds(c * points, points)
        return pltpu.make_async_copy(out_s.at[:, span], out_hbm.at[:, span], out_sem.at[c])

    for c in range(steps):
        for copy in loads(c):
            copy.start()
    for c in range(steps):
        for copy in loads(c):
            copy.wait()
        span = pl.ds(c * some, some)
        total = fore_s[span].astype(F32) + inc_s[span].astype(F32)
        total = jnp.swapaxes(total.reshape(points, members, LANES), 0, 1)
        out_s[:, pl.ds(c * points, points), :] = total.astype(BF16)
        store(c).start()
    for c in range(steps):
        store(c).wait()


def finish(fore, inc, members):
    tiles, rows, _ = fore.shape
    shape = (members, tiles * rows // members, LANES)
    steps = 8
    hbm = pl.BlockSpec(memory_space=pl.ANY)
    return pl.pallas_call(
        finish_kernel,
        out_shape=jax.ShapeDtypeStruct(shape, BF16),
        in_specs=[hbm, hbm],
        out_specs=hbm,
        scratch_shapes=[
            pltpu.VMEM(fore.shape, BF16),
            pltpu.VMEM(fore.shape, BF16),
            pltpu.VMEM(shape, BF16),
            pltpu.SemaphoreType.DMA((2 * steps,)),
            pltpu.SemaphoreType.DMA((steps,)),
        ],
        compiler_params=pltpu.CompilerParams(vmem_limit_bytes=40 * 2**20),
        name="finish",
    )(fore, inc)


def neighbours(inner, outer, axis, wrap):
    count = lax.axis_size(axis)
    within = [(i, i ^ 1) for i in range(count)]
    links = [(i, (i + 1) % count) for i in range(1, count if wrap else count - 1, 2)]
    across = links + [(b, a) for a, b in links]
    got = lax.ppermute(outer, axis, across)
    return lax.ppermute(inner, axis, within), got


def swapped(index, low, high, odd):
    moved = jnp.where(index < low, index + high, jnp.where(index >= high, index - high, index))
    return jnp.where(odd == 1, moved, index)


def exchange(blocks):
    return lax.all_to_all(blocks, MR, split_axis=0, concat_axis=0, tiled=True)


def shards(
    latent_vertex_values,
    background_field,
    edge_senders,
    grid_parent,
    w_send,
    w_recv,
    w_node,
    w_agg,
    w_out,
    norm_gain,
    w_dec,
    obs_loc,
    obs_count,
    obs_value,
    obs_var,
    obs_nbr,
    loc_weight,
):
    members, nodes, width = latent_vertex_values.shape
    grid_r = background_field.shape[1]
    groups, regions = lax.axis_size("member"), lax.axis_size("region")

    def node_major(array):
        return array.transpose(1, 0, 2).reshape(-1, array.shape[2])

    odd = lax.axis_index("region") % 2

    def rim(start):
        return node_major(lax.dynamic_slice_in_dim(latent_vertex_values, start, RIM, 1))

    inner, outer = neighbours(
        rim(jnp.where(odd == 1, 0, nodes - RIM)),
        rim(jnp.where(odd == 1, nodes - RIM, 0)),
        "region",
        True,
    )
    edges = swapped(edge_senders - (nodes - RIM), RIM, nodes + RIM, odd)
    weights = (w_send, w_node, w_agg, w_out, norm_gain[None], w_dec)
    processed, fore = forecast(
        project(latent_vertex_values, w_send, w_recv),
        outer,
        inner,
        background_field,
        edges,
        grid_parent,
        weights,
    )
    processed = processed.reshape(nodes, members, width).transpose(1, 0, 2)
    ens = exchange(fore)
    ens = ens.reshape(groups, regions, *ens.shape[1:])
    payload = observe(ens, obs_loc, obs_count, obs_value, obs_var)
    pay_inner, pay_outer = neighbours(payload, payload, MR, False)
    slots = obs_loc.shape[0]
    nbr = swapped(obs_nbr, slots, 2 * slots, odd)
    inc = analyse(pay_outer, payload, pay_inner, nbr, loc_weight, ens)
    landed = exchange(inc.reshape(groups * regions, *inc.shape[2:]))
    return processed, finish(fore, landed, members)


def solution(mesh):
    in_specs = (
        P("member", "region", None),
        P("member", "region", None),
        P("region", None),
        P("region"),
        P(),
        P(),
        P(),
        P(),
        P(),
        P(),
        P(),
        P(MR),
        P(MR),
        P(MR),
        P(MR),
        P(None, MR),
        P(None, MR),
    )
    out_specs = (P("member", "region", None), P("member", "region", None))
    return jax.shard_map(shards, mesh=mesh, in_specs=in_specs, out_specs=out_specs, check_vma=False)
```
